128 devices in a mesh: wide: 32 (over x, y, z_lo), narrow: 4 (over z_hi, core).
Axes of the slice: x: 4, y: 4, z: 4 (z_hi: 2, z_lo: 2; z = z_hi * 2 + z_lo), core: 2. Of those that a mesh axis runs over, the one named last changes fastest.
Arguments:
- queries: bfloat16 [98304, 768], P(('wide', 'narrow')), may hold values from -24 to 24
- labels: bfloat16 [98304, 768], P(('wide', 'narrow')), may hold values from -24 to 24
- logit_scale: float32 [1], replicated, may hold values from 2 to 3
Outputs:
- loss: float32 [98304], P(('wide', 'narrow'))
- query_grad: bfloat16 [98304, 768], P(('wide', 'narrow'))
- label_grad: bfloat16 [98304, 768], P(('wide', 'narrow'))
The draws below stay inside these ranges and needn't reach their ends.
All inputs are finite; a program needn't handle non-finite values.
Results may differ from the reference program's by a relative error of at most 0.004.
Values may be sent and summed in bfloat16 or wider, within the bound.
A program may use at most 128 MiB of HBM per device.

```python
import math
import jax
import jax.numpy as jnp
from jax import lax

D = 768
TOK_DEV = 768
TOKENS = 98304
N_WIDE = 32
N_NARROW = 4


def shared_base(key):
    return jax.random.normal(key, (TOKENS, D), jnp.float32)


def draw_labels(key, part):
    base = shared_base(key)
    values = base
    return jnp.clip(values, -24.0, 24.0).astype(jnp.bfloat16)


def draw_queries(key, part):
    key = jax.random.fold_in(key, 11)
    first = jax.random.fold_in(key, 0)
    values = jax.random.normal(first, (TOKENS, D), jnp.float32)
    return jnp.clip(values, -24.0, 24.0).astype(jnp.bfloat16)


def setup_inputs(seed: int = 0) -> dict:
    arg_keys = jax.random.split(jax.random.key(seed), 4)
    queries = draw_queries(jax.random.fold_in(arg_keys[3], 71), 0)
    labels = draw_labels(jax.random.fold_in(arg_keys[3], 71), 0)
    logit_scale = jnp.clip(jax.random.uniform(arg_keys[2], (1,), jnp.float32, 2.0, 3.0), 2.0, 3.0)
    return dict(queries=queries, labels=labels, logit_scale=logit_scale)


def reference(queries, labels, logit_scale):
    block = TOK_DEV * N_NARROW
    query_blocks = queries.reshape(N_WIDE, block, D)
    label_blocks = labels.reshape(N_WIDE, block, D)
    prev_blocks = jnp.roll(label_blocks, 1, axis=0)
    factor = logit_scale[0] / math.sqrt(D)

    def one_block(items):
        query_rows, own_labels, prev_labels = items
        window = jnp.concatenate([own_labels, prev_labels], axis=0)
        scores = jnp.dot(query_rows, window.T, preferred_element_type=jnp.float32) * factor
        top = lax.optimization_barrier(jnp.max(scores, axis=1, keepdims=True))
        lse = top[:, 0] + jnp.log(lax.optimization_barrier(jnp.sum(jnp.exp(scores - top), axis=1)))
        columns = jnp.arange(2 * block, dtype=jnp.int32)
        positive = jnp.arange(block, dtype=jnp.int32)
        hit = columns[None, :] == positive[:, None]
        loss = lse - lax.optimization_barrier(jnp.sum(jnp.where(hit, scores, 0.0), axis=1))
        weights = (jnp.exp(scores - lse[:, None]) - hit.astype(jnp.float32)).astype(jnp.bfloat16)
        query_grad = jnp.dot(weights, window, preferred_element_type=jnp.float32).astype(jnp.bfloat16)
        terms = jnp.dot(weights.T, query_rows, preferred_element_type=jnp.float32)
        return (loss, query_grad, terms[:block], terms[block:])
    loss, query_grad, own_terms, prev_terms = lax.map(one_block, (query_blocks, label_blocks, prev_blocks))
    label_grad = own_terms + jnp.roll(prev_terms, -1, axis=0)
    return (loss.reshape(TOKENS), query_grad.reshape(TOKENS, D), label_grad.reshape(TOKENS, D).astype(jnp.bfloat16))
```

```python
import functools
import math

import jax
import jax.numpy as jnp
from jax import lax
from jax.experimental import pallas as pl
from jax.experimental.pallas import tpu as pltpu
from jax.sharding import PartitionSpec as P

MESH = pl.DeviceIdType.MESH
F32, BF16 = jnp.float32, jnp.bfloat16
CH = 256
SUB = 64
NT = (((1,), (1,)), ((), ()))
NN = (((1,), (0,)), ((), ()))
TN = (((0,), (0,)), ((), ()))


def kernel(
    scale_ref, q_ref, l_ref, loss_ref, qg_ref, lg_ref,
    QB, LB, E, MX, SM, AL, ST, RS, SII, ACC, QGT, QG0,
    YS, LS, QS, DS3, DS1, YR, LR, QR, DR2, DR0, QO, LO,
    s_in, s_out, s_q, r_q, s_l, r_l, s_y, r_y, s_1, r_1, s_3, r_3, s_st, r_st,
    s_yr, r_yr, s_d3, r_d3, s_qz, r_qz, s_lz, r_lz, s_d1, r_d1,
):
    rows = q_ref.shape[0]
    nk, ns = rows // CH, rows // SUB
    per = CH // SUB
    w, n = lax.axis_index("wide"), lax.axis_index("narrow")
    nw = lax.axis_size("wide")
    par = lax.rem(w, 2)
    wx = w + 1 - 2 * par
    nc = n + 1 - 2 * lax.rem(n, 2)
    dev_q, dev_l = (wx, n), (wx, lax.rem(n + 2, 4))
    dev_d, dev_qd = (w, nc), (wx, nc)
    dev_yf, dev_yb = (lax.rem(w + 2, nw), n), (lax.rem(w + nw - 2, nw), n)
    even, odd = par == 0, par == 1
    factor = scale_ref[0] * (1.0 / math.sqrt(q_ref.shape[1]))

    def sub(i):
        return pl.ds(pl.multiple_of(i * SUB, SUB), SUB)

    def chunk(c):
        return pl.ds(pl.multiple_of(c * CH, CH), CH)

    def rc(src, dst, ssem, rsem, dev):
        return pltpu.make_async_remote_copy(
            src_ref=src, dst_ref=dst, send_sem=ssem, recv_sem=rsem, device_id=dev, device_id_type=MESH
        )

    def c_q(i):
        return rc(q_ref.at[sub(i)], QB.at[2, sub(i)], s_q.at[i], r_q.at[i], dev_q)

    def c_l(i):
        return rc(l_ref.at[sub(i)], LB.at[1, sub(i)], s_l.at[i], r_l.at[i], dev_l)

    def c_y(i):
        return rc(LB.at[1 - par, sub(i)], LB.at[2, sub(i)], s_y.at[i], r_y.at[i], dev_yf)

    def c_1():
        return rc(q_ref, QB.at[1], s_1.at[0], r_1.at[0], dev_d)

    def c_3(i):
        return rc(QB.at[2, sub(i)], QB.at[3, sub(i)], s_3.at[i], r_3.at[i], dev_d)

    def c_st(j):
        return rc(ST, RS.at[j], s_st.at[j], r_st.at[j], (dev_d, dev_q, dev_qd)[j])

    def c_yr(i):
        return rc(YS.at[sub(i)], YR.at[sub(i)], s_yr.at[i], r_yr.at[i], dev_yb)

    def c_d3(c):
        return rc(DS3.at[chunk(c)], DR2.at[chunk(c)], s_d3.at[c], r_d3.at[c], dev_d)

    def c_d1(c):
        return rc(DS1.at[chunk(c)], DR0.at[chunk(c)], s_d1.at[c], r_d1.at[c], dev_d)

    def c_qz(i):
        return rc(QS.at[sub(i)], QR.at[sub(i)], s_qz.at[i], r_qz.at[i], dev_q)

    def c_lz(i):
        return rc(LS.at[sub(i)], LR.at[sub(i)], s_lz.at[i], r_lz.at[i], dev_l)

    def loop(lo, hi, body):
        def step(i, carry):
            body(i)
            return carry

        lax.fori_loop(lo, hi, step, 0)

    barrier = pltpu.get_barrier_semaphore()
    for dev in (dev_q, dev_l, dev_yf, dev_yb, dev_d, dev_qd):
        pl.semaphore_signal(barrier, inc=1, device_id=dev, device_id_type=MESH)
    in_q = pltpu.make_async_copy(q_ref, QB.at[0], s_in.at[0])
    in_l = pltpu.make_async_copy(l_ref, LB.at[0], s_in.at[1])
    in_q.start()
    in_l.start()
    in_q.wait()
    in_l.wait()
    pl.semaphore_wait(barrier, 6)

    def send_first(i):
        c_l(i).start()
        c_q(i).start()

        @pl.when(odd)
        def _():
            c_y(i).start()

    loop(0, ns, send_first)
    c_1().start()

    def slot_of(t):
        return jnp.where(t == 0, 0, jnp.where(t == 1, 2 - par, jnp.where(t == 2, 1, 2 * par)))

    def put(ts, k, cols, d):
        m = jnp.max(d, axis=0, keepdims=True)
        e = jnp.exp(d - m)
        E[ts, chunk(k), cols] = e
        MX[ts, pl.ds(k, 1), cols] = m
        SM[ts, pl.ds(k, 1), cols] = jnp.sum(e, axis=0, keepdims=True)

    def narrow_piece(s, k, c):
        for t in (2, 3):
            lab = LB[slot_of(t), chunk(k), :]
            d = lax.dot_general(lab, QB[2 + s, chunk(c), :], NT, preferred_element_type=F32) * factor
            put(2 * t + s, k, chunk(c), d)

    def wide(t, s, k):
        lab = LB[slot_of(t), chunk(k), :]
        d = lax.dot_general(lab, QB[2 * (t // 2) + s], NT, preferred_element_type=F32) * factor
        put(2 * t + s, k, slice(None), d)

        @pl.when((t == 0) & (s == 0))
        def _():
            row = lax.broadcasted_iota(jnp.int32, (CH, rows), 0) + k * CH
            col = lax.broadcasted_iota(jnp.int32, (CH, rows), 1)
            SII[pl.ds(k, 1), :] = jnp.sum(jnp.where(row == col, d, 0.0), axis=0, keepdims=True)

    ACC[...] = jnp.zeros_like(ACC)

    def phase1(x):
        k, j = x // 4, lax.rem(x, 4)

        @pl.when(k < nk)
        def _():
            c_l(x).wait_recv()

            @pl.when(even)
            def _():
                c_y(x).start()

            c_q(x).wait_recv()
            c_3(x).start()

        @pl.when((k == 0) & (j == 1))
        def _():
            c_1().wait_recv()

        @pl.when((k > 0) & (j < 2))
        def _():
            @pl.when(j == 1)
            def _():
                loop((k - 1) * per, k * per, lambda i: c_3(i).wait_recv())

            @pl.when((j == 0) & odd)
            def _():
                loop((k - 1) * per, k * per, lambda i: c_y(i).wait_recv())

            kk = k - 1
            m = jnp.where(k == nk, kk, 2 * kk + 1)
            loop(0, m, lambda i: narrow_piece(j, jnp.minimum(i, kk), jnp.where(i < kk, kk, i - kk)))

        @pl.when((k > 0) & (j == 2) & even)
        def _():
            loop((k - 1) * per, k * per, lambda i: c_y(i).wait_recv())

        lo = jnp.where(k == 0, jnp.where(j == 0, 0, j + 2), 0)
        cnt = jnp.where(
            k == 0, jnp.where(j == 0, 3, 1), jnp.where(j >= 2, 1, jnp.where(k == nk, 2, 0))
        )

        def piece(i):
            t = jnp.where(k == 0, 0, jnp.where(j >= 2, 1, 2 + i))
            s = jnp.where(k == 0, (lo + i) // 3, lax.rem(j, 2))
            kk = jnp.where(k == 0, lax.rem(lo + i, 3), k - 1)
            wide(t, s, kk)

        loop(0, cnt, piece)

    loop(0, 4 * (nk + 1), phase1)

    for s in range(4):
        p, h = s // 2, s % 2
        parts = [(2 * (2 * p + tt) + h, k) for tt in range(2) for k in range(nk)]
        m = functools.reduce(jnp.maximum, [MX[ts, k : k + 1, :] for ts, k in parts])
        total = sum(SM[ts, k : k + 1, :] * jnp.exp(MX[ts, k : k + 1, :] - m) for ts, k in parts)
        ST[s : s + 1, :] = m
        ST[4 + s : 5 + s, :] = total
    for j in range(3):
        c_st(j).start()
    for j in range(3):
        c_st(j).wait_recv()
    for s in range(4):
        p, h = s // 2, s % 2
        ms = [ST[s : s + 1, :]] + [RS[j, s ^ (j + 1) : (s ^ (j + 1)) + 1, :] for j in range(3)]
        ls = [ST[4 + s : 5 + s, :]] + [RS[j, 4 + (s ^ (j + 1)) : 5 + (s ^ (j + 1)), :] for j in range(3)]
        top = functools.reduce(jnp.maximum, ms)
        lse = top + jnp.log(sum(a * jnp.exp(b - top) for a, b in zip(ls, ms)))
        for tt in range(2):
            ts = 2 * (2 * p + tt) + h
            for k in range(nk):
                AL[ts, k : k + 1, :] = jnp.exp(MX[ts, k : k + 1, :] - lse)
        if s == 0:
            loss_ref[...] = lse - sum(SII[k : k + 1, :] for k in range(nk))

    def lg_piece(t, c):
        row = lax.broadcasted_iota(jnp.int32, (CH, rows), 0) + c * CH
        col = lax.broadcasted_iota(jnp.int32, (CH, rows), 1) + rows * jnp.minimum(t, 1)
        hit = jnp.where(row == col, 1.0, 0.0)
        w0 = (E[2 * t, chunk(c), :] * AL[2 * t, pl.ds(c, 1), :] - hit).astype(BF16)
        w1 = (E[2 * t + 1, chunk(c), :] * AL[2 * t + 1, pl.ds(c, 1), :]).astype(BF16)
        qs = 2 * (t // 2)
        g = lax.dot_general(w0, QB[qs], NN, preferred_element_type=F32)
        g = g + lax.dot_general(w1, QB[qs + 1], NN, preferred_element_type=F32)
        slot = slot_of(t)
        ACC[slot, chunk(c), :] = ACC[slot, chunk(c), :] + g

    def qg_piece(s, c):
        p, h = s // 2, lax.rem(s, 2)
        row = lax.broadcasted_iota(jnp.int32, (CH, CH), 0)
        col = lax.broadcasted_iota(jnp.int32, (CH, CH), 1) + c * CH + rows * jnp.minimum(s, 1)
        total = None
        for tt in range(2):
            t = 2 * p + tt
            ws = []
            for k in range(nk):
                x = E[2 * t + h, chunk(k), chunk(c)] * AL[2 * t + h, k : k + 1, chunk(c)]
                if tt == 0:
                    x = x - jnp.where(row + k * CH == col, 1.0, 0.0)
                ws.append(x.astype(BF16))
            g = lax.dot_general(jnp.concatenate(ws, axis=0), LB[slot_of(t)], TN, preferred_element_type=F32)
            total = g if total is None else total + g
        QGT[...] = total

    def service(i):
        c_yr(i).wait_recv()

        @pl.when(even)
        def _():
            LS[sub(i), :] = (ACC[1, sub(i), :] + YR[sub(i), :].astype(F32)).astype(BF16)
            c_lz(i).start()

    def phase3(x):
        first = x < 5 * nk
        y = x - 5 * nk
        c = jnp.where(first, x // 5, y // 3)
        v = jnp.where(first, lax.rem(x, 5), 5 + lax.rem(y + 3 * nk, 3))
        is_lg = (v == 0) | ((v >= 3) & (v <= 5))
        t = jnp.where(v == 0, 1 + 2 * par, jnp.where(v == 3, 2, jnp.where(v == 4, 3 - 2 * par, 0)))
        s = jnp.where(v == 1, 3, jnp.where(v == 2, 2, jnp.where(v == 6, 1, 0)))

        @pl.when(is_lg)
        def _():
            lg_piece(t, c)

        @pl.when(jnp.logical_not(is_lg))
        def _():
            qg_piece(s, c)

        @pl.when(v == 0)
        def _():
            YS[chunk(c), :] = ACC[2, chunk(c), :].astype(BF16)
            loop(c * per, (c + 1) * per, lambda i: c_yr(i).start())

        @pl.when(v == 1)
        def _():
            DS3[chunk(c), :] = QGT[...].astype(BF16)
            c_d3(c).start()

        @pl.when(v == 2)
        def _():
            c_d3(c).wait_recv()
            QS[chunk(c), :] = (QGT[...] + DR2[chunk(c), :].astype(F32)).astype(BF16)
            loop(c * per, (c + 1) * per, lambda i: c_qz(i).start())

        @pl.when((v == 4) & odd)
        def _():
            LS[chunk(c), :] = ACC[1, chunk(c), :].astype(BF16)
            loop(c * per, (c + 1) * per, lambda i: c_lz(i).start())

        @pl.when(v == 6)
        def _():
            DS1[chunk(c), :] = QGT[...].astype(BF16)
            c_d1(c).start()

        @pl.when(v == 7)
        def _():
            QG0[chunk(c), :] = QGT[...]

        @pl.when((x >= 5) & (lax.rem(x, 2) == 1))
        def _():
            service((x - 5) // 2)

    steps = 8 * nk
    loop(0, steps, phase3)
    loop((steps - 4) // 2, ns, service)
    loop(0, nk, lambda c: c_d1(c).wait_recv())

    def finish(i):
        c_qz(i).wait_recv()
        g = QG0[sub(i), :] + DR0[sub(i), :].astype(F32)
        QO[sub(i), :] = (g + QR[sub(i), :].astype(F32)).astype(BF16)
        pltpu.make_async_copy(QO.at[sub(i)], qg_ref.at[sub(i)], s_out.at[0]).start()
        c_lz(i).wait_recv()
        back = jnp.where(odd, YR[sub(i), :].astype(F32), 0.0)
        LO[sub(i), :] = (ACC[0, sub(i), :] + back + LR[sub(i), :].astype(F32)).astype(BF16)
        pltpu.make_async_copy(LO.at[sub(i)], lg_ref.at[sub(i)], s_out.at[1]).start()

    loop(0, ns, finish)

    def drain(i):
        for copy in (c_q, c_l, c_y, c_3, c_yr, c_qz, c_lz):
            copy(i).wait_send()

    loop(0, ns, drain)
    c_1().wait_send()
    for j in range(3):
        c_st(j).wait_send()

    def drain_cores(c):
        c_d3(c).wait_send()
        c_d1(c).wait_send()

    loop(0, nk, drain_cores)
    pltpu.make_async_copy(QO, qg_ref, s_out.at[0]).wait()
    pltpu.make_async_copy(LO, lg_ref, s_out.at[1]).wait()


def local(queries, labels, logit_scale):
    rows, width = queries.shape
    nk, ns = rows // CH, rows // SUB
    block = (rows, width)
    dma = pltpu.SemaphoreType.DMA
    loss, query_grad, label_grad = pl.pallas_call(
        kernel,
        out_shape=(
            jax.ShapeDtypeStruct((1, rows), F32),
            jax.ShapeDtypeStruct(block, BF16),
            jax.ShapeDtypeStruct(block, BF16),
        ),
        in_specs=[
            pl.BlockSpec(memory_space=pltpu.SMEM),
            pl.BlockSpec(memory_space=pl.ANY),
            pl.BlockSpec(memory_space=pl.ANY),
        ],
        out_specs=(
            pl.BlockSpec(memory_space=pltpu.VMEM),
            pl.BlockSpec(memory_space=pl.ANY),
            pl.BlockSpec(memory_space=pl.ANY),
        ),
        scratch_shapes=[
            pltpu.VMEM((4, *block), BF16),
            pltpu.VMEM((3, *block), BF16),
            pltpu.VMEM((8, rows, rows), F32),
            pltpu.VMEM((8, 8, rows), F32),
            pltpu.VMEM((8, 8, rows), F32),
            pltpu.VMEM((8, 8, rows), F32),
            pltpu.VMEM((8, rows), F32),
            pltpu.VMEM((3, 8, rows), F32),
            pltpu.VMEM((8, rows), F32),
            pltpu.VMEM((3, *block), F32),
            pltpu.VMEM((CH, width), F32),
            pltpu.VMEM(block, F32),
            *[pltpu.VMEM(block, BF16)] * 12,
            dma((2,)), dma((2,)),
            dma((ns,)), dma((ns,)),
            dma((ns,)), dma((ns,)),
            dma((ns,)), dma((ns,)),
            dma((1,)), dma((1,)),
            dma((ns,)), dma((ns,)),
            dma((3,)), dma((3,)),
            dma((ns,)), dma((ns,)),
            dma((nk,)), dma((nk,)),
            dma((ns,)), dma((ns,)),
            dma((ns,)), dma((ns,)),
            dma((nk,)), dma((nk,)),
        ],
        compiler_params=pltpu.CompilerParams(
            collective_id=0, has_side_effects=True, vmem_limit_bytes=62 * 2**20
        ),
        cost_estimate=pl.CostEstimate(
            flops=6 * rows * 8 * rows * width, bytes_accessed=8 * rows * width, transcendentals=8 * rows * rows
        ),
    )(logit_scale, queries, labels)
    return loss.reshape(rows), query_grad, label_grad


def solution(mesh):
    in_specs = (P(("wide", "narrow"), None), P(("wide", "narrow"), None), P())
    out_specs = (P(("wide", "narrow")), P(("wide", "narrow"), None), P(("wide", "narrow"), None))
    return jax.shard_map(local, mesh=mesh, in_specs=in_specs, out_specs=out_specs, check_vma=False)
```

```python
import functools
import math

import jax
import jax.numpy as jnp
from jax import lax
from jax.experimental import pallas as pl
from jax.experimental.pallas import tpu as pltpu
from jax.sharding import PartitionSpec as P

MESH = pl.DeviceIdType.MESH
F32, BF16 = jnp.float32, jnp.bfloat16
CH = 256
SUB = 64
NT = (((1,), (1,)), ((), ()))
NN = (((1,), (0,)), ((), ()))
TN = (((0,), (0,)), ((), ()))
OWN_Q, GOT_Q, PASSED, OWN_L, GOT_L = 0, 2, 4, 6, 7


def kernel(
    scale_ref, q_ref, l_ref, loss_ref, qg_ref, lg_ref,
    B, E, MX, SM, AL, SA, SB, RA, RB, SII, TR, ACC, QG0, GT,
    YS, LS, QS, DS3, DS5, DS1, YR, LR, QR, DR2, DR4, DR0,
    s_in, s_q, r_q, s_l, r_l, s_y, r_y, s_1, r_1, s_3, r_3, s_5, r_5, s_sa, r_sa, s_sb, r_sb,
    s_yr, r_yr, s_qz, r_qz, s_lz, r_lz, s_d3, r_d3, s_d5, r_d5, s_d1, r_d1,
):
    rows = q_ref.shape[0]
    nk, ns = rows // CH, rows // SUB
    per = CH // SUB
    w, n = lax.axis_index("wide"), lax.axis_index("narrow")
    nw = lax.axis_size("wide")
    par = lax.rem(w, 2)
    even, odd = par == 0, par == 1
    wx = w + 1 - 2 * par
    nc = n + 1 - 2 * lax.rem(n, 2)

    def at(step):
        return lax.rem(w + nw + step, nw)

    dev_q, dev_l = (wx, n), (wx, lax.rem(n + 2, 4))
    dev_d, dev_qd = (w, nc), (wx, nc)
    out_y = (at(4 * par - 2), n)
    back_y = (at(2 - 4 * par), n)
    factor = scale_ref[0] * (1.0 / math.sqrt(q_ref.shape[1]))

    def sub(i):
        return pl.ds(pl.multiple_of(i * SUB, SUB), SUB)

    def chunk(c):
        return pl.ds(pl.multiple_of(c * CH, CH), CH)

    def rc(src, dst, ssem, rsem, dev):
        return pltpu.make_async_remote_copy(
            src_ref=src, dst_ref=dst, send_sem=ssem, recv_sem=rsem, device_id=dev, device_id_type=MESH
        )

    def c_q(i):
        return rc(q_ref.at[sub(i)], B.at[GOT_Q, sub(i)], s_q.at[i], r_q.at[i], dev_q)

    def c_l(i):
        return rc(l_ref.at[sub(i)], B.at[GOT_L, sub(i)], s_l.at[i], r_l.at[i], dev_l)

    def c_y(i):
        return rc(B.at[OWN_L * par, sub(i)], B.at[PASSED, sub(i)], s_y.at[i], r_y.at[i], out_y)

    def c_1():
        return rc(q_ref, B.at[OWN_Q + 1], s_1.at[0], r_1.at[0], dev_d)

    def c_3(i):
        return rc(B.at[GOT_Q, sub(i)], B.at[GOT_Q + 1, sub(i)], s_3.at[i], r_3.at[i], dev_d)

    def c_5(i):
        return rc(B.at[PASSED, sub(i)], B.at[PASSED + 1, sub(i)], s_5.at[i], r_5.at[i], dev_d)

    def c_sa(j, dev):
        return rc(SA, RA.at[j], s_sa.at[j], r_sa.at[j], dev)

    def c_sb(i, j, dev):
        return rc(SB, RB.at[j], s_sb.at[i], r_sb.at[j], dev)

    def c_yr(i):
        return rc(YS.at[sub(i)], YR.at[sub(i)], s_yr.at[i], r_yr.at[i], back_y)

    def c_qz(i):
        return rc(QS.at[sub(i)], QR.at[sub(i)], s_qz.at[i], r_qz.at[i], dev_q)

    def c_lz(i):
        return rc(LS.at[sub(i)], LR.at[sub(i)], s_lz.at[i], r_lz.at[i], dev_l)

    def c_d3(c):
        return rc(DS3.at[chunk(c)], DR2.at[chunk(c)], s_d3.at[c], r_d3.at[c], dev_d)

    def c_d5(c):
        return rc(DS5.at[chunk(c)], DR4.at[chunk(c)], s_d5.at[c], r_d5.at[c], dev_d)

    def c_d1(c):
        return rc(DS1.at[chunk(c)], DR0.at[chunk(c)], s_d1.at[c], r_d1.at[c], dev_d)

    def loop(lo, hi, body):
        def step(i, carry):
            body(i)
            return carry

        lax.fori_loop(lo, hi, step, 0)

    in_q = pltpu.make_async_copy(q_ref, B.at[OWN_Q], s_in.at[0])
    in_l = pltpu.make_async_copy(l_ref, B.at[OWN_L], s_in.at[1])
    in_q.start()
    in_l.start()
    barrier = pltpu.get_barrier_semaphore()
    for dev in (back_y, out_y, dev_l, dev_q, dev_qd, dev_d):
        pl.semaphore_signal(barrier, inc=1, device_id=dev, device_id_type=MESH)
    in_q.wait()
    in_l.wait()
    pl.semaphore_wait(barrier, 6)

    def send_first(i):
        c_y(i).start()
        c_l(i).start()
        c_q(i).start()

    loop(0, ns, send_first)
    c_1().start()

    def labels_of(t):
        return jnp.where(t == 0, OWN_L, jnp.where(t == 3, OWN_L - 2 * par, GOT_L))

    def queries_of(t):
        return jnp.where(t == 0, OWN_Q, jnp.where(t == 1, PASSED - PASSED * par, GOT_Q))

    def scores(t, h, row0, height, col0, width):
        lab = B[labels_of(t), pl.ds(row0, height), :]
        qry = B[queries_of(t) + h, pl.ds(col0, width), :]
        return lax.dot_general(lab, qry, NT, preferred_element_type=F32) * factor

    def put(ts, k, cols, d):
        m = jnp.max(d, axis=0, keepdims=True)
        e = jnp.exp(d - m)
        E[ts, chunk(k), cols] = e
        MX[k, pl.ds(ts, 1), cols] = m
        SM[k, pl.ds(ts, 1), cols] = jnp.sum(e, axis=0, keepdims=True)

    def own_piece(h, k):
        d = scores(0, h, pl.multiple_of(k * CH, CH), CH, 0, rows)
        put(h, k, slice(None), d)

        @pl.when(h == 0)
        def _():
            row = lax.broadcasted_iota(jnp.int32, (CH, rows), 0) + k * CH
            col = lax.broadcasted_iota(jnp.int32, (CH, rows), 1)
            SII[pl.ds(k, 1), :] = jnp.sum(jnp.where(row == col, d, 0.0), axis=0, keepdims=True)

    def square_piece(h, k, c):
        for t in (1, 2, 3):
            d = scores(t, h, pl.multiple_of(k * CH, CH), CH, pl.multiple_of(c * CH, CH), CH)
            put(2 * t + h, k, chunk(c), d)

    def take_in(i):
        c_q(i).wait_recv()
        c_3(i).start()
        c_y(i).wait_recv()

        @pl.when(even)
        def _():
            c_5(i).start()

    def arrived(lo, hi):
        loop(lo, hi, lambda i: c_3(i).wait_recv())

        @pl.when(even)
        def _():
            loop(lo, hi, lambda i: c_5(i).wait_recv())

    def phase1(x):
        k, j = x // 8, lax.rem(x, 8)
        i, h, kk = lax.rem(j, 3), j // 3, k - 1
        loop(x * per // 8, (x + 1) * per // 8, take_in)

        @pl.when((k == 0) & (j == 3))
        def _():
            c_1().wait_recv()

        @pl.when((k == 0) & (j < 6))
        def _():
            own_piece(h, i)

        @pl.when((k > 0) & (j == 0))
        def _():
            loop(kk * per, k * per, lambda i: c_l(i).wait_recv())

        @pl.when((k > 0) & (j == 3))
        def _():
            arrived(kk * per, k * per)

        @pl.when((k > 0) & (j < 6) & (i < 2 * kk + 1))
        def _():
            square_piece(h, jnp.minimum(i, kk), jnp.where(i < kk, kk, i - kk))

    loop(0, 8 * nk, phase1)
    loop((nk - 1) * per, ns, lambda i: c_l(i).wait_recv())
    edge = (nk - 1) * CH

    def last_pieces(h):
        @pl.when(h == 1)
        def _():
            arrived((nk - 1) * per, ns)

        for t in (1, 2, 3):
            d = scores(t, h, 0, rows, edge, CH)
            for k in range(nk):
                put(2 * t + h, k, slice(edge, rows), d[k * CH : (k + 1) * CH])
        for t in (1, 2, 3):
            put(2 * t + h, nk - 1, slice(0, edge), scores(t, h, edge, CH, 0, edge))

    loop(0, 2, last_pieces)

    def lg_piece(t0, count, c):
        def term(i):
            t = t0 + i
            row = lax.broadcasted_iota(jnp.int32, (CH, rows), 0) + c * CH
            col = lax.broadcasted_iota(jnp.int32, (CH, rows), 1) + rows * jnp.minimum(t, 1)
            hit = jnp.where(row == col, 1.0, 0.0)
            w0 = (E[2 * t, chunk(c), :] * AL[c, pl.ds(2 * t, 1), :] - hit).astype(BF16)
            w1 = (E[2 * t + 1, chunk(c), :] * AL[c, pl.ds(2 * t + 1, 1), :]).astype(BF16)
            g = lax.dot_general(w0, B[queries_of(t)], NN, preferred_element_type=F32)
            g = g + lax.dot_general(w1, B[queries_of(t) + 1], NN, preferred_element_type=F32)

            @pl.when(i == 0)
            def _():
                GT[...] = g

            @pl.when(i > 0)
            def _():
                GT[...] = GT[...] + g

        loop(0, count, term)

    def qg_piece(t0, count, h, c):
        def term(i):
            t = t0 + i
            ts = 2 * t + h
            row = lax.broadcasted_iota(jnp.int32, (CH, CH), 0)
            col = lax.broadcasted_iota(jnp.int32, (CH, CH), 1) + c * CH + rows * jnp.minimum(ts, 1)
            ws = []
            for k in range(nk):
                x = E[ts, chunk(k), chunk(c)] * AL[k, pl.ds(ts, 1), chunk(c)]
                ws.append((x - jnp.where(row + k * CH == col, 1.0, 0.0)).astype(BF16))
            g = lax.dot_general(
                jnp.concatenate(ws, axis=0), B[labels_of(t)], TN, preferred_element_type=F32
            )

            @pl.when(i == 0)
            def _():
                GT[...] = g

            @pl.when(i > 0)
            def _():
                GT[...] = GT[...] + g

        loop(0, count, term)

    def join(*parts):
        top = functools.reduce(jnp.maximum, parts)
        return top + jnp.log(sum(jnp.exp(part - top) for part in parts))

    m = functools.reduce(jnp.maximum, [MX[k] for k in range(nk)])
    of_term = m + jnp.log(sum(SM[k] * jnp.exp(MX[k] - m) for k in range(nk)))
    third = of_term[2:4]
    SA[0:2, :] = jnp.where(odd, join(of_term[0:2], third), of_term[0:2])
    SA[2:4, :] = join(of_term[4:6], of_term[6:8])
    SB[...] = third

    def near():
        return [c_sa(0, dev_d), c_sa(1, dev_q), c_sa(2, dev_qd)]

    def far_even():
        return [
            c_sb(1, 1, (at(3), n)), c_sb(2, 2, (at(3), nc)), c_sb(3, 1, (at(2), n)), c_sb(4, 2, (at(2), nc)),
            c_sa(5, (at(-2), n)), c_sa(6, (at(-2), nc)), c_sb(0, 0, dev_d),
        ]

    def far_odd():
        return [c_sa(3, (at(-3), n)), c_sa(4, (at(-3), nc))]

    def each(copies, act):
        for copy in copies:
            act(copy)

    pl.when(even)(lambda: each(far_even(), lambda copy: copy.start()))
    pl.when(odd)(lambda: each(far_odd(), lambda copy: copy.start()))
    each(near(), lambda copy: copy.start())

    got = SA[2:4, :]
    own_view = jnp.concatenate([of_term[0:4], got, got], axis=0)
    for k in range(nk):
        AL[k] = jnp.exp(MX[k] - own_view)

    def early(i):
        of_got = lax.rem(i, 2) == 0

        @pl.when(of_got | even)
        def _():
            qg_piece(jnp.where(of_got, 2, 1), jnp.where(of_got, 2, 1), 1 - i // 2, 0)

        @pl.when(i == 0)
        def _():
            DS3[:CH, :] = GT[...].astype(BF16)
            c_d3(0).start()

        @pl.when((i == 1) & even)
        def _():
            DS5[:CH, :] = GT[...].astype(BF16)
            c_d5(0).start()

        @pl.when((i == 2) | ((i == 3) & even))
        def _():
            QG0[chunk(i - 2), :] = GT[...]

    loop(0, 4, early)

    def swap(x):
        return jnp.concatenate([x[1:2], x[0:1]], axis=0)

    each(near(), lambda copy: copy.wait_recv())
    for j in (1, 2):
        c_sb(j, j, dev_d).wait_recv()

    @pl.when(even)
    def _():
        for j in (3, 4, 5, 6):
            c_sa(j, dev_d).wait_recv()
        c_sb(0, 0, dev_d).wait_recv()

    far = [RB[1], swap(RB[2])]
    near0 = [SA[0:2, :], swap(RA[0, 0:2, :]), RA[1, 2:4, :], swap(RA[2, 2:4, :])]
    near1 = [SA[2:4, :], swap(RA[0, 2:4, :]), RA[1, 0:2, :], swap(RA[2, 0:2, :])]

    def settle(lse0, lse1, lse2):
        lse = jnp.concatenate([lse0, lse2, lse1, lse1], axis=0)
        for k in range(nk):
            AL[k] = jnp.exp(MX[k] - lse)
        loss_ref[...] = lse0[0:1] - sum(SII[k : k + 1, :] for k in range(nk))
        TR[0:1, :] = jnp.exp(SA[2:3, :CH] - lse1[0:1, :CH])
        TR[1:2, :] = jnp.exp(RA[0, 3:4, :CH] - lse1[0:1, :CH])
        TR[2:3, :] = jnp.exp(SB[0:1, :CH] - lse2[0:1, :CH])

    @pl.when(even)
    def _():
        of_passed = [SB[...], swap(RB[0]), RA[5, 0:2, :], swap(RA[6, 0:2, :]), RA[3, 2:4, :], swap(RA[4, 2:4, :])]
        lse2 = join(*of_passed)
        settle(join(*near0, *far), join(*near1), lse2)
        TR[3:4, :] = jnp.exp(RB[0, 1:2, :CH] - lse2[0:1, :CH])

    @pl.when(odd)
    def _():
        lse0 = join(*near0)
        settle(lse0, join(*near1, *far), lse0)

    def send(copy, c):
        loop(c * per, (c + 1) * per, lambda i: copy(i).start())

    column = jnp.transpose(TR[...])
    c_d3(0).wait_recv()
    QS[:CH, :] = (QG0[:CH, :] * column[:, 0:1] + DR2[:CH, :].astype(F32) * column[:, 1:2]).astype(BF16)
    send(c_qz, 0)

    @pl.when(even)
    def _():
        c_d5(0).wait_recv()
        g = QG0[CH : 2 * CH, :] * column[:, 2:3] + DR4[:CH, :].astype(F32) * column[:, 3:4]
        YS[:CH, :] = g.astype(BF16)
        send(c_yr, 0)

    def phase3(x):
        first = x < 5 * nk
        y = x - 5 * nk
        c = jnp.where(first, x // 5, y // 4)
        v = jnp.where(first, lax.rem(x, 5), 6 + lax.rem(y + 8 * nk, 4))
        lg = (v == 2) | (v == 7) | ((v == 1) & odd) | ((v == 8) & even)
        later = (c > 0) | (v >= 6)
        qg = later & ((v == 0) | (v == 3) | (v == 6) | (v == 9) | (((v == 1) | (v == 4)) & even))

        @pl.when(lg)
        def _():
            t0 = jnp.where(v == 2, 1, jnp.where(v == 7, 0, 3))
            lg_piece(t0, jnp.where(v == 2, 2, 1), c)

        @pl.when(qg)
        def _():
            passed = (v == 1) | (v == 4)
            t0 = jnp.where(passed, 1, jnp.where(v >= 6, 0, 2))
            count = jnp.where(passed, 1, jnp.where(v >= 6, 1 + par, 2))
            qg_piece(t0, count, jnp.where((v == 0) | (v == 1) | (v == 6), 1, 0), c)

        @pl.when((v == 0) & later)
        def _():
            DS3[chunk(c), :] = GT[...].astype(BF16)
            c_d3(c).start()

        @pl.when((v == 1) & even & later)
        def _():
            DS5[chunk(c), :] = GT[...].astype(BF16)
            c_d5(c).start()

        @pl.when((v == 1) & odd)
        def _():
            YS[chunk(c), :] = GT[...].astype(BF16)
            send(c_yr, c)

        @pl.when(v == 2)
        def _():
            LS[chunk(c), :] = GT[...].astype(BF16)
            send(c_lz, c)

        @pl.when((v == 3) & later)
        def _():
            c_d3(c).wait_recv()
            QS[chunk(c), :] = (GT[...] + DR2[chunk(c), :].astype(F32)).astype(BF16)
            send(c_qz, c)

        @pl.when((v == 4) & even & later)
        def _():
            c_d5(c).wait_recv()
            YS[chunk(c), :] = (GT[...] + DR4[chunk(c), :].astype(F32)).astype(BF16)
            send(c_yr, c)

        @pl.when(v == 6)
        def _():
            DS1[chunk(c), :] = GT[...].astype(BF16)
            c_d1(c).start()

        @pl.when(v == 7)
        def _():
            ACC[chunk(c), :] = GT[...]

        @pl.when((v == 8) & even)
        def _():
            ACC[chunk(c), :] = ACC[chunk(c), :] + GT[...]

        @pl.when(v == 9)
        def _():
            QG0[chunk(c), :] = GT[...]

    loop(0, 9 * nk, phase3)
    loop(0, nk, lambda c: c_d1(c).wait_recv())

    def finish(i):
        c_yr(i).wait_recv()
        passed = YR[sub(i), :].astype(F32)
        c_qz(i).wait_recv()
        g = QG0[sub(i), :] + DR0[sub(i), :].astype(F32) + jnp.where(even, passed, 0.0)
        qg_ref[sub(i), :] = (g + QR[sub(i), :].astype(F32)).astype(BF16)
        c_lz(i).wait_recv()
        g = ACC[sub(i), :] + jnp.where(odd, passed, 0.0)
        lg_ref[sub(i), :] = (g + LR[sub(i), :].astype(F32)).astype(BF16)

    loop(0, ns, finish)

    def drain(i):
        for copy in (c_q, c_l, c_y, c_3, c_yr, c_qz, c_lz):
            copy(i).wait_send()

        @pl.when(even)
        def _():
            c_5(i).wait_send()

    loop(0, ns, drain)
    c_1().wait_send()
    each(near(), lambda copy: copy.wait_send())
    pl.when(even)(lambda: each(far_even(), lambda copy: copy.wait_send()))
    pl.when(odd)(lambda: each(far_odd(), lambda copy: copy.wait_send()))

    def drain_cores(c):
        c_d3(c).wait_send()
        c_d1(c).wait_send()

        @pl.when(even)
        def _():
            c_d5(c).wait_send()

    loop(0, nk, drain_cores)


def local(queries, labels, logit_scale):
    rows, width = queries.shape
    nk, ns = rows // CH, rows // SUB
    block = (rows, width)
    dma = pltpu.SemaphoreType.DMA
    counts = [ns, ns, ns, 1, ns, ns, 7, 5, ns, ns, ns, nk, nk, nk]
    loss, query_grad, label_grad = pl.pallas_call(
        kernel,
        out_shape=(
            jax.ShapeDtypeStruct((1, rows), F32),
            jax.ShapeDtypeStruct(block, BF16),
            jax.ShapeDtypeStruct(block, BF16),
        ),
        in_specs=[
            pl.BlockSpec(memory_space=pltpu.SMEM),
            pl.BlockSpec(memory_space=pltpu.HBM),
            pl.BlockSpec(memory_space=pltpu.HBM),
        ],
        out_specs=(pl.BlockSpec(memory_space=pltpu.VMEM),) * 3,
        scratch_shapes=[
            pltpu.VMEM((8, *block), BF16),
            pltpu.VMEM((8, rows, rows), F32),
            pltpu.VMEM((nk, 8, rows), F32),
            pltpu.VMEM((nk, 8, rows), F32),
            pltpu.VMEM((nk, 8, rows), F32),
            pltpu.VMEM((4, rows), F32),
            pltpu.VMEM((2, rows), F32),
            pltpu.VMEM((7, 4, rows), F32),
            pltpu.VMEM((3, 2, rows), F32),
            pltpu.VMEM((8, rows), F32),
            pltpu.VMEM((8, CH), F32),
            pltpu.VMEM(block, F32),
            pltpu.VMEM(block, F32),
            pltpu.VMEM((CH, width), F32),
            *[pltpu.VMEM(block, BF16)] * 12,
            dma((2,)),
            *[dma((count,)) for count in counts for _ in range(2)],
        ],
        compiler_params=pltpu.CompilerParams(
            collective_id=0, has_side_effects=True, vmem_limit_bytes=51 * 2**20
        ),
        cost_estimate=pl.CostEstimate(
            flops=6 * rows * 8 * rows * width, bytes_accessed=8 * rows * width, transcendentals=8 * rows * rows
        ),
    )(logit_scale, queries, labels)
    return loss.reshape(rows), query_grad, label_grad


def solution(mesh):
    in_specs = (P(("wide", "narrow"), None), P(("wide", "narrow"), None), P())
    out_specs = (P(("wide", "narrow")), P(("wide", "narrow"), None), P(("wide", "narrow"), None))
    return jax.shard_map(local, mesh=mesh, in_specs=in_specs, out_specs=out_specs, check_vma=False)
```

```python
import functools
import math

import jax
import jax.numpy as jnp
from jax import lax
from jax.experimental import pallas as pl
from jax.experimental.pallas import tpu as pltpu
from jax.sharding import PartitionSpec as P

MESH = pl.DeviceIdType.MESH
F32, BF16 = jnp.float32, jnp.bfloat16
CH = 256
SUB = 128
NT = (((1,), (1,)), ((), ()))
NN = (((1,), (0,)), ((), ()))
TN = (((0,), (0,)), ((), ()))
OWN_Q, GOT_Q, PASSED, OWN_L, GOT_L = 0, 2, 4, 6, 7


def kernel(
    scale_ref, q_ref, l_ref, loss_ref, qg_ref, lg_ref,
    B, E, MX, SM, AL, SA, SB, RA, RB, SII, TR, ACC, QG0, GT,
    YS, LS, QS, DS3, DS5, DS1, YR, LR, QR, DR2, DR4, DR0,
    s_in, s_q, r_q, s_l, r_l, s_y, r_y, s_1, r_1, s_3, r_3, s_5, r_5, s_sa, r_sa, s_sb, r_sb,
    s_yr, r_yr, s_qz, r_qz, s_lz, r_lz, s_d3, r_d3, s_d5, r_d5, s_d1, r_d1,
):
    rows = q_ref.shape[0]
    nk, ns = rows // CH, rows // SUB
    per = CH // SUB
    w, n = lax.axis_index("wide"), lax.axis_index("narrow")
    nw = lax.axis_size("wide")
    par = lax.rem(w, 2)
    even, odd = par == 0, par == 1
    wx = w + 1 - 2 * par
    nc = n + 1 - 2 * lax.rem(n, 2)

    def at(step):
        return lax.rem(w + nw + step, nw)

    dev_q, dev_l = (wx, n), (wx, lax.rem(n + 2, 4))
    dev_d, dev_qd = (w, nc), (wx, nc)
    out_y = (at(4 * par - 2), n)
    back_y = (at(2 - 4 * par), n)
    factor = scale_ref[0] * (1.0 / math.sqrt(q_ref.shape[1]))

    def sub(i):
        return pl.ds(pl.multiple_of(i * SUB, SUB), SUB)

    def chunk(c):
        return pl.ds(pl.multiple_of(c * CH, CH), CH)

    def rc(src, dst, ssem, rsem, dev):
        return pltpu.make_async_remote_copy(
            src_ref=src, dst_ref=dst, send_sem=ssem, recv_sem=rsem, device_id=dev, device_id_type=MESH
        )

    def c_q(i):
        return rc(q_ref.at[sub(i)], B.at[GOT_Q, sub(i)], s_q.at[i], r_q.at[i], dev_q)

    def c_l(i):
        return rc(l_ref.at[sub(i)], B.at[GOT_L, sub(i)], s_l.at[i], r_l.at[i], dev_l)

    def c_y(i):
        return rc(B.at[OWN_L * par, sub(i)], B.at[PASSED, sub(i)], s_y.at[i], r_y.at[i], out_y)

    def c_1():
        return rc(q_ref, B.at[OWN_Q + 1], s_1.at[0], r_1.at[0], dev_d)

    def c_3(i):
        return rc(B.at[GOT_Q, sub(i)], B.at[GOT_Q + 1, sub(i)], s_3.at[i], r_3.at[i], dev_d)

    def c_5(i):
        return rc(B.at[PASSED, sub(i)], B.at[PASSED + 1, sub(i)], s_5.at[i], r_5.at[i], dev_d)

    def c_sa(j, dev):
        return rc(SA, RA.at[j], s_sa.at[j], r_sa.at[j], dev)

    def c_sb(i, j, dev):
        return rc(SB, RB.at[j], s_sb.at[i], r_sb.at[j], dev)

    def c_yr(i):
        return rc(YS.at[sub(i)], YR.at[sub(i)], s_yr.at[i], r_yr.at[i], back_y)

    def c_qz(i):
        return rc(QS.at[sub(i)], QR.at[sub(i)], s_qz.at[i], r_qz.at[i], dev_q)

    def c_lz(i):
        return rc(LS.at[sub(i)], LR.at[sub(i)], s_lz.at[i], r_lz.at[i], dev_l)

    def c_d3(c):
        return rc(DS3.at[chunk(c)], DR2.at[chunk(c)], s_d3.at[c], r_d3.at[c], dev_d)

    def c_d5(c):
        return rc(DS5.at[chunk(c)], DR4.at[chunk(c)], s_d5.at[c], r_d5.at[c], dev_d)

    def c_d1(c):
        return rc(DS1.at[chunk(c)], DR0.at[chunk(c)], s_d1.at[c], r_d1.at[c], dev_d)

    def loop(lo, hi, body):
        def step(i, carry):
            body(i)
            return carry

        lax.fori_loop(lo, hi, step, 0)

    in_q = pltpu.make_async_copy(q_ref, B.at[OWN_Q], s_in.at[0])
    in_l = pltpu.make_async_copy(l_ref, B.at[OWN_L], s_in.at[1])
    in_q.start()
    in_l.start()
    barrier = pltpu.get_barrier_semaphore()
    for dev in (back_y, out_y, dev_l, dev_q, dev_qd, dev_d):
        pl.semaphore_signal(barrier, inc=1, device_id=dev, device_id_type=MESH)
    in_q.wait()
    in_l.wait()
    pl.semaphore_wait(barrier, 6)

    def send_first(i):
        c_y(i).start()
        c_l(i).start()
        c_q(i).start()

    loop(0, ns, send_first)
    c_1().start()

    def labels_of(t):
        return jnp.where(t == 0, OWN_L, jnp.where(t == 3, OWN_L - 2 * par, GOT_L))

    def queries_of(t):
        return jnp.where(t == 0, OWN_Q, jnp.where(t == 1, PASSED - PASSED * par, GOT_Q))

    def scores(t, h, row0, height, col0, width):
        lab = B[labels_of(t), pl.ds(row0, height), :]
        qry = B[queries_of(t) + h, pl.ds(col0, width), :]
        return lax.dot_general(lab, qry, NT, preferred_element_type=F32) * factor

    def put(ts, k, cols, d):
        m = jnp.max(d, axis=0, keepdims=True)
        e = jnp.exp(d - m)
        E[ts, chunk(k), cols] = e
        MX[k, pl.ds(ts, 1), cols] = m
        SM[k, pl.ds(ts, 1), cols] = jnp.sum(e, axis=0, keepdims=True)

    def own_piece(h, k):
        d = scores(0, h, pl.multiple_of(k * CH, CH), CH, 0, rows)
        put(h, k, slice(None), d)

        @pl.when(h == 0)
        def _():
            row = lax.broadcasted_iota(jnp.int32, (CH, rows), 0) + k * CH
            col = lax.broadcasted_iota(jnp.int32, (CH, rows), 1)
            SII[pl.ds(k, 1), :] = jnp.sum(jnp.where(row == col, d, 0.0), axis=0, keepdims=True)

    def square_piece(h, k, c):
        for t in (1, 2, 3):
            d = scores(t, h, pl.multiple_of(k * CH, CH), CH, pl.multiple_of(c * CH, CH), CH)
            put(2 * t + h, k, chunk(c), d)

    def take_in(i):
        c_q(i).wait_recv()
        c_3(i).start()
        c_y(i).wait_recv()

        @pl.when(even)
        def _():
            c_5(i).start()

    def arrived(lo, hi):
        loop(lo, hi, lambda i: c_3(i).wait_recv())

        @pl.when(even)
        def _():
            loop(lo, hi, lambda i: c_5(i).wait_recv())

    def phase1(x):
        k, j = x // 8, lax.rem(x, 8)
        i, h, kk = lax.rem(j, 3), j // 3, k - 1
        loop(x * per // 8, (x + 1) * per // 8, take_in)

        @pl.when((k == 0) & (j == 3))
        def _():
            c_1().wait_recv()

        @pl.when((k == 0) & (j < 6))
        def _():
            own_piece(h, i)

        @pl.when((k > 0) & (j == 0))
        def _():
            loop(kk * per, k * per, lambda i: c_l(i).wait_recv())

        @pl.when((k > 0) & (j == 3))
        def _():
            arrived(kk * per, k * per)

        @pl.when((k > 0) & (j < 6) & (i < 2 * kk + 1))
        def _():
            square_piece(h, jnp.minimum(i, kk), jnp.where(i < kk, kk, i - kk))

    loop(0, 8 * nk, phase1)
    edge = (nk - 1) * CH

    def last_queries(h, upto):
        for t in (1, 2, 3):
            d = scores(t, h, 0, upto, edge, CH)
            for k in range(upto // CH):
                put(2 * t + h, k, slice(edge, rows), d[k * CH : (k + 1) * CH])

    def last_labels(h, upto):
        for t in (1, 2, 3):
            put(2 * t + h, nk - 1, slice(0, upto), scores(t, h, edge, CH, 0, upto))

    last_queries(0, edge)
    loop((nk - 1) * per, ns, lambda i: c_l(i).wait_recv())
    last_labels(0, rows)
    last_labels(1, edge)
    arrived((nk - 1) * per, ns)
    last_queries(1, rows)

    def lg_piece(t0, count, c, more=False):
        def term(i):
            t = t0 + i
            row = lax.broadcasted_iota(jnp.int32, (CH, rows), 0) + c * CH
            col = lax.broadcasted_iota(jnp.int32, (CH, rows), 1) + rows * jnp.minimum(t, 1)
            hit = jnp.where(row == col, 1.0, 0.0)
            w0 = (E[2 * t, chunk(c), :] * AL[c, pl.ds(2 * t, 1), :] - hit).astype(BF16)
            w1 = (E[2 * t + 1, chunk(c), :] * AL[c, pl.ds(2 * t + 1, 1), :]).astype(BF16)
            g = lax.dot_general(w0, B[queries_of(t)], NN, preferred_element_type=F32)
            g = g + lax.dot_general(w1, B[queries_of(t) + 1], NN, preferred_element_type=F32)
            if more:
                GT[...] = GT[...] + g
                return

            @pl.when(i == 0)
            def _():
                GT[...] = g

            @pl.when(i > 0)
            def _():
                GT[...] = GT[...] + g

        loop(0, count, term)

    def qg_piece(t0, count, h, c):
        def term(i):
            t = t0 + i
            ts = 2 * t + h
            row = lax.broadcasted_iota(jnp.int32, (CH, CH), 0)
            col = lax.broadcasted_iota(jnp.int32, (CH, CH), 1) + c * CH + rows * jnp.minimum(ts, 1)
            ws = []
            for k in range(nk):
                x = E[ts, chunk(k), chunk(c)] * AL[k, pl.ds(ts, 1), chunk(c)]
                ws.append((x - jnp.where(row + k * CH == col, 1.0, 0.0)).astype(BF16))
            g = lax.dot_general(
                jnp.concatenate(ws, axis=0), B[labels_of(t)], TN, preferred_element_type=F32
            )

            @pl.when(i == 0)
            def _():
                GT[...] = g

            @pl.when(i > 0)
            def _():
                GT[...] = GT[...] + g

        loop(0, count, term)

    def join(*parts):
        top = functools.reduce(jnp.maximum, parts)
        return top + jnp.log(sum(jnp.exp(part - top) for part in parts))

    m = functools.reduce(jnp.maximum, [MX[k] for k in range(nk)])
    of_term = m + jnp.log(sum(SM[k] * jnp.exp(MX[k] - m) for k in range(nk)))
    third = of_term[2:4]
    SA[0:2, :] = jnp.where(odd, join(of_term[0:2], third), of_term[0:2])
    SA[2:4, :] = join(of_term[4:6], of_term[6:8])
    SB[...] = third

    def near():
        return [c_sa(0, dev_d), c_sa(1, dev_q), c_sa(2, dev_qd)]

    def far_even():
        return [
            c_sb(1, 1, (at(3), n)), c_sb(2, 2, (at(3), nc)), c_sb(3, 1, (at(2), n)), c_sb(4, 2, (at(2), nc)),
            c_sa(5, (at(-2), n)), c_sa(6, (at(-2), nc)), c_sb(0, 0, dev_d),
        ]

    def far_odd():
        return [c_sa(3, (at(-3), n)), c_sa(4, (at(-3), nc))]

    def each(copies, act):
        for copy in copies:
            act(copy)

    pl.when(even)(lambda: each(far_even(), lambda copy: copy.start()))
    pl.when(odd)(lambda: each(far_odd(), lambda copy: copy.start()))
    each(near(), lambda copy: copy.start())

    got = SA[2:4, :]
    own_view = jnp.concatenate([of_term[0:4], got, got], axis=0)
    for k in range(nk):
        AL[k] = jnp.exp(MX[k] - own_view)

    def early(i):
        of_got = lax.rem(i, 2) == 0

        @pl.when(of_got | even)
        def _():
            qg_piece(jnp.where(of_got, 2, 1), jnp.where(of_got, 2, 1), 1 - i // 2, 0)

        @pl.when(i == 0)
        def _():
            DS3[:CH, :] = GT[...].astype(BF16)
            c_d3(0).start()

        @pl.when((i == 1) & even)
        def _():
            DS5[:CH, :] = GT[...].astype(BF16)
            c_d5(0).start()

        @pl.when((i == 2) | ((i == 3) & even))
        def _():
            QG0[chunk(i - 2), :] = GT[...]

    loop(0, 4, early)

    def swap(x):
        return jnp.concatenate([x[1:2], x[0:1]], axis=0)

    def settle(first, pairs):
        lse = jnp.concatenate(pairs, axis=0)
        last = first + lse.shape[0]
        for k in range(nk):
            AL[k, first:last, :] = jnp.exp(MX[k, first:last, :] - lse)

    def send(copy, c):
        loop(c * per, (c + 1) * per, lambda i: copy(i).start())

    each(near(), lambda copy: copy.wait_recv())
    near0 = [SA[0:2, :], swap(RA[0, 0:2, :]), RA[1, 2:4, :], swap(RA[2, 2:4, :])]
    near1 = [SA[2:4, :], swap(RA[0, 2:4, :]), RA[1, 0:2, :], swap(RA[2, 0:2, :])]

    @pl.when(even)
    def _():
        lse1 = join(*near1)
        settle(4, [lse1, lse1])
        TR[4:6, :] = lse1[:, :CH]

    @pl.when(odd)
    def _():
        lse0 = join(*near0)
        settle(0, [lse0, lse0])
        loss_ref[...] = (lse0[0:1] - sum(SII[k : k + 1, :] for k in range(nk))).reshape(rows)

    lg_piece(2 - par, 1, 0)

    for j in (1, 2):
        c_sb(j, j, dev_d).wait_recv()
    far = [RB[1], swap(RB[2])]

    @pl.when(even)
    def _():
        for j in (3, 4, 5, 6):
            c_sa(j, dev_d).wait_recv()
        c_sb(0, 0, dev_d).wait_recv()
        lse0 = join(*near0, *far)
        lse2 = join(SB[...], swap(RB[0]), RA[5, 0:2, :], swap(RA[6, 0:2, :]), RA[3, 2:4, :], swap(RA[4, 2:4, :]))
        settle(0, [lse0, lse2])
        loss_ref[...] = (lse0[0:1] - sum(SII[k : k + 1, :] for k in range(nk))).reshape(rows)
        TR[2:3, :] = jnp.exp(SB[0:1, :CH] - lse2[0:1, :CH])
        TR[3:4, :] = jnp.exp(RB[0, 1:2, :CH] - lse2[0:1, :CH])

    @pl.when(odd)
    def _():
        lse1 = join(*near1, *far)
        settle(4, [lse1, lse1])
        TR[4:6, :] = lse1[:, :CH]

    lg_piece(1 + par, 1, 0, more=True)
    LS[:CH, :] = GT[...].astype(BF16)
    send(c_lz, 0)

    TR[0:1, :] = jnp.exp(SA[2:3, :CH] - TR[4:5, :])
    TR[1:2, :] = jnp.exp(RA[0, 3:4, :CH] - TR[4:5, :])
    column = jnp.transpose(TR[...])
    c_d3(0).wait_recv()
    QS[:CH, :] = (QG0[:CH, :] * column[:, 0:1] + DR2[:CH, :].astype(F32) * column[:, 1:2]).astype(BF16)
    send(c_qz, 0)

    @pl.when(even)
    def _():
        c_d5(0).wait_recv()
        g = QG0[CH : 2 * CH, :] * column[:, 2:3] + DR4[:CH, :].astype(F32) * column[:, 3:4]
        YS[:CH, :] = g.astype(BF16)
        send(c_yr, 0)

    def phase3(x):
        first = x < 5 * nk
        y = x - 5 * nk
        c = jnp.where(first, x // 5, y // 4)
        v = jnp.where(first, lax.rem(x, 5), 6 + lax.rem(y + 8 * nk, 4))
        later = (c > 0) | (v >= 6)
        lg = ((v == 2) & later) | (v == 7) | ((v == 1) & odd) | ((v == 8) & even)
        qg = later & ((v == 0) | (v == 3) | (v == 6) | (v == 9) | (((v == 1) | (v == 4)) & even))

        @pl.when(lg)
        def _():
            t0 = jnp.where(v == 2, 1, jnp.where(v == 7, 0, 3))
            lg_piece(t0, jnp.where(v == 2, 2, 1), c)

        @pl.when(qg)
        def _():
            passed = (v == 1) | (v == 4)
            t0 = jnp.where(passed, 1, jnp.where(v >= 6, 0, 2))
            count = jnp.where(passed, 1, jnp.where(v >= 6, 1 + par, 2))
            qg_piece(t0, count, jnp.where((v == 0) | (v == 1) | (v == 6), 1, 0), c)

        @pl.when((v == 0) & later)
        def _():
            DS3[chunk(c), :] = GT[...].astype(BF16)
            c_d3(c).start()

        @pl.when((v == 1) & even & later)
        def _():
            DS5[chunk(c), :] = GT[...].astype(BF16)
            c_d5(c).start()

        @pl.when((v == 1) & odd)
        def _():
            YS[chunk(c), :] = GT[...].astype(BF16)
            send(c_yr, c)

        @pl.when((v == 2) & later)
        def _():
            LS[chunk(c), :] = GT[...].astype(BF16)
            send(c_lz, c)

        @pl.when((v == 3) & later)
        def _():
            c_d3(c).wait_recv()
            QS[chunk(c), :] = (GT[...] + DR2[chunk(c), :].astype(F32)).astype(BF16)
            send(c_qz, c)

        @pl.when((v == 4) & even & later)
        def _():
            c_d5(c).wait_recv()
            YS[chunk(c), :] = (GT[...] + DR4[chunk(c), :].astype(F32)).astype(BF16)
            send(c_yr, c)

        @pl.when(v == 6)
        def _():
            DS1[chunk(c), :] = GT[...].astype(BF16)
            c_d1(c).start()

        @pl.when(v == 7)
        def _():
            ACC[chunk(c), :] = GT[...]

        @pl.when((v == 8) & even)
        def _():
            ACC[chunk(c), :] = ACC[chunk(c), :] + GT[...]

        @pl.when(v == 9)
        def _():
            QG0[chunk(c), :] = GT[...]

    loop(0, 9 * nk, phase3)
    loop(0, nk, lambda c: c_d1(c).wait_recv())

    def finish(i):
        c_yr(i).wait_recv()
        passed = YR[sub(i), :].astype(F32)
        c_qz(i).wait_recv()
        g = QG0[sub(i), :] + DR0[sub(i), :].astype(F32) + jnp.where(even, passed, 0.0)
        qg_ref[sub(i), :] = (g + QR[sub(i), :].astype(F32)).astype(BF16)
        c_lz(i).wait_recv()
        g = ACC[sub(i), :] + jnp.where(odd, passed, 0.0)
        lg_ref[sub(i), :] = (g + LR[sub(i), :].astype(F32)).astype(BF16)

    loop(0, ns, finish)

    def drain(i):
        for copy in (c_q, c_l, c_y, c_3, c_yr, c_qz, c_lz):
            copy(i).wait_send()

        @pl.when(even)
        def _():
            c_5(i).wait_send()

    loop(0, ns, drain)
    c_1().wait_send()
    each(near(), lambda copy: copy.wait_send())
    pl.when(even)(lambda: each(far_even(), lambda copy: copy.wait_send()))
    pl.when(odd)(lambda: each(far_odd(), lambda copy: copy.wait_send()))

    def drain_cores(c):
        c_d3(c).wait_send()
        c_d1(c).wait_send()

        @pl.when(even)
        def _():
            c_d5(c).wait_send()

    loop(0, nk, drain_cores)


def hand_over_kernel(*refs):
    ins, outs, sems = refs[:3], refs[3:6], refs[6]
    copies = [pltpu.make_async_copy(src, dst, sems.at[i]) for i, (src, dst) in enumerate(zip(ins, outs))]
    for copy in copies:
        copy.start()
    for copy in copies:
        copy.wait()


def hand_over(*results):
    return pl.pallas_call(
        hand_over_kernel,
        out_shape=tuple(jax.ShapeDtypeStruct(x.shape, x.dtype) for x in results),
        in_specs=[pl.BlockSpec(memory_space=pltpu.VMEM)] * 3,
        out_specs=(pl.BlockSpec(memory_space=pltpu.HBM),) * 3,
        scratch_shapes=[pltpu.SemaphoreType.DMA((3,))],
        compiler_params=pltpu.CompilerParams(vmem_limit_bytes=4 * 2**20),
    )(*results)


def local(queries, labels, logit_scale):
    rows, width = queries.shape
    nk, ns = rows // CH, rows // SUB
    block = (rows, width)
    dma = pltpu.SemaphoreType.DMA
    counts = [ns, ns, ns, 1, ns, ns, 7, 5, ns, ns, ns, nk, nk, nk]
    loss, query_grad, label_grad = pl.pallas_call(
        kernel,
        out_shape=(
            jax.ShapeDtypeStruct((rows,), F32),
            jax.ShapeDtypeStruct(block, BF16),
            jax.ShapeDtypeStruct(block, BF16),
        ),
        in_specs=[
            pl.BlockSpec(memory_space=pltpu.SMEM),
            pl.BlockSpec(memory_space=pltpu.HBM),
            pl.BlockSpec(memory_space=pltpu.HBM),
        ],
        out_specs=(pl.BlockSpec(memory_space=pltpu.VMEM),) * 3,
        scratch_shapes=[
            pltpu.VMEM((8, *block), BF16),
            pltpu.VMEM((8, rows, rows), F32),
            pltpu.VMEM((nk, 8, rows), F32),
            pltpu.VMEM((nk, 8, rows), F32),
            pltpu.VMEM((nk, 8, rows), F32),
            pltpu.VMEM((4, rows), F32),
            pltpu.VMEM((2, rows), F32),
            pltpu.VMEM((7, 4, rows), F32),
            pltpu.VMEM((3, 2, rows), F32),
            pltpu.VMEM((8, rows), F32),
            pltpu.VMEM((8, CH), F32),
            pltpu.VMEM(block, F32),
            pltpu.VMEM(block, F32),
            pltpu.VMEM((CH, width), F32),
            *[pltpu.VMEM(block, BF16)] * 12,
            dma((2,)),
            *[dma((count,)) for count in counts for _ in range(2)],
        ],
        compiler_params=pltpu.CompilerParams(
            collective_id=0, has_side_effects=True, vmem_limit_bytes=51 * 2**20
        ),
        cost_estimate=pl.CostEstimate(
            flops=6 * rows * 8 * rows * width, bytes_accessed=8 * rows * width, transcendentals=8 * rows * rows
        ),
    )(logit_scale, queries, labels)
    return hand_over(loss, query_grad, label_grad)


def solution(mesh):
    in_specs = (P(("wide", "narrow"), None), P(("wide", "narrow"), None), P())
    out_specs = (P(("wide", "narrow")), P(("wide", "narrow"), None), P(("wide", "narrow"), None))
    return jax.shard_map(local, mesh=mesh, in_specs=in_specs, out_specs=out_specs, check_vma=False)
```

```python
import functools
import math

import jax
import jax.numpy as jnp
from jax import lax
from jax.experimental import pallas as pl
from jax.experimental.pallas import tpu as pltpu
from jax.sharding import PartitionSpec as P

MESH = pl.DeviceIdType.MESH
F32, BF16 = jnp.float32, jnp.bfloat16
CH = 256
SUB = 128
PARTS = 4
NT = (((1,), (1,)), ((), ()))
NN = (((1,), (0,)), ((), ()))
TN = (((0,), (0,)), ((), ()))
OWN_Q, GOT_Q, PASSED, OWN_L, GOT_L = 0, 2, 4, 6, 7


def kernel(
    scale_ref, q_ref, l_ref, loss_ref, qg_ref, lg_ref,
    B, E, MX, SM, AL, SA, SB, SP, RA, RB, RP, SII, TR, ACC, QG0, GT,
    YS, LS, QS, DS3, DS5, DS1, YR, LR, QR, DR2, DR4, DR0,
    s_in, s_q, r_q, s_l, r_l, s_y, r_y, s_1, r_1, s_3, r_3, s_5, r_5, s_sa, r_sa, s_sb, r_sb, s_sp, r_sp,
    s_yr, r_yr, s_qz, r_qz, s_lz, r_lz, s_d3, r_d3, s_d5, r_d5, s_d1, r_d1,
):
    rows = q_ref.shape[0]
    nk, ns = rows // CH, rows // SUB
    per = CH // SUB
    w, n = lax.axis_index("wide"), lax.axis_index("narrow")
    nw = lax.axis_size("wide")
    par = lax.rem(w, 2)
    even, odd = par == 0, par == 1
    wx = w + 1 - 2 * par
    nc = n + 1 - 2 * lax.rem(n, 2)

    def at(step):
        return lax.rem(w + nw + step, nw)

    dev_q, dev_l = (wx, n), (wx, lax.rem(n + 2, 4))
    dev_d, dev_qd = (w, nc), (wx, nc)
    out_y = (at(4 * par - 2), n)
    back_y = (at(2 - 4 * par), n)
    factor = scale_ref[0] * (1.0 / math.sqrt(q_ref.shape[1]))

    def sub(i):
        return pl.ds(pl.multiple_of(i * SUB, SUB), SUB)

    def chunk(c):
        return pl.ds(pl.multiple_of(c * CH, CH), CH)

    def rc(src, dst, ssem, rsem, dev):
        return pltpu.make_async_remote_copy(
            src_ref=src, dst_ref=dst, send_sem=ssem, recv_sem=rsem, device_id=dev, device_id_type=MESH
        )

    def c_q(i):
        return rc(q_ref.at[sub(i)], B.at[GOT_Q, sub(i)], s_q.at[i], r_q.at[i], dev_q)

    def c_l(i):
        return rc(l_ref.at[sub(i)], B.at[GOT_L, sub(i)], s_l.at[i], r_l.at[i], dev_l)

    def c_y(i):
        return rc(B.at[OWN_L * par, sub(i)], B.at[PASSED, sub(i)], s_y.at[i], r_y.at[i], out_y)

    def c_1():
        return rc(q_ref, B.at[OWN_Q + 1], s_1.at[0], r_1.at[0], dev_d)

    def c_3(i):
        return rc(B.at[GOT_Q, sub(i)], B.at[GOT_Q + 1, sub(i)], s_3.at[i], r_3.at[i], dev_d)

    def c_5(i):
        return rc(B.at[PASSED, sub(i)], B.at[PASSED + 1, sub(i)], s_5.at[i], r_5.at[i], dev_d)

    def c_sa(j, dev):
        return rc(SA, RA.at[j], s_sa.at[j], r_sa.at[j], dev)

    def c_sp(i, j, dev):
        return rc(SP, RP.at[j], s_sp.at[i], r_sp.at[j], dev)

    def c_sb(i, j, dev):
        return rc(SB, RB.at[j], s_sb.at[i], r_sb.at[j], dev)

    def c_yr(i):
        return rc(YS.at[sub(i)], YR.at[sub(i)], s_yr.at[i], r_yr.at[i], back_y)

    def c_qz(i):
        return rc(QS.at[sub(i)], QR.at[sub(i)], s_qz.at[i], r_qz.at[i], dev_q)

    def c_lz(i):
        return rc(LS.at[sub(i)], LR.at[sub(i)], s_lz.at[i], r_lz.at[i], dev_l)

    def c_d3(c):
        return rc(DS3.at[chunk(c)], DR2.at[chunk(c)], s_d3.at[c], r_d3.at[c], dev_d)

    def c_d5(c):
        return rc(DS5.at[chunk(c)], DR4.at[chunk(c)], s_d5.at[c], r_d5.at[c], dev_d)

    def c_d1(c):
        return rc(DS1.at[chunk(c)], DR0.at[chunk(c)], s_d1.at[c], r_d1.at[c], dev_d)

    def loop(lo, hi, body):
        def step(i, carry):
            body(i)
            return carry

        lax.fori_loop(lo, hi, step, 0)

    in_q = pltpu.make_async_copy(q_ref, B.at[OWN_Q], s_in.at[0])
    in_l = pltpu.make_async_copy(l_ref, B.at[OWN_L], s_in.at[1])
    in_q.start()
    in_l.start()
    barrier = pltpu.get_barrier_semaphore()
    for dev in (back_y, out_y, dev_l, dev_q, dev_qd, dev_d):
        pl.semaphore_signal(barrier, inc=1, device_id=dev, device_id_type=MESH)
    in_q.wait()
    in_l.wait()
    pl.semaphore_wait(barrier, 6)

    def send_first(i):
        c_y(i).start()
        c_l(i).start()
        c_q(i).start()

    loop(0, ns, send_first)
    c_1().start()

    def labels_of(t):
        return jnp.where(t == 0, OWN_L, jnp.where(t == 3, OWN_L - 2 * par, GOT_L))

    def queries_of(t):
        return jnp.where(t == 0, OWN_Q, jnp.where(t == 1, PASSED - PASSED * par, GOT_Q))

    def scores(t, h, row0, height, col0, width):
        lab = B[labels_of(t), pl.ds(row0, height), :]
        qry = B[queries_of(t) + h, pl.ds(col0, width), :]
        return lax.dot_general(lab, qry, NT, preferred_element_type=F32) * factor

    def put(ts, k, cols, d):
        m = jnp.max(d, axis=0, keepdims=True)
        e = jnp.exp(d - m)
        E[ts, chunk(k), cols] = e
        MX[k, pl.ds(ts, 1), cols] = m
        SM[k, pl.ds(ts, 1), cols] = jnp.sum(e, axis=0, keepdims=True)

    def own_piece(h, k):
        d = scores(0, h, pl.multiple_of(k * CH, CH), CH, 0, rows)
        put(h, k, slice(None), d)

        @pl.when(h == 0)
        def _():
            row = lax.broadcasted_iota(jnp.int32, (CH, rows), 0) + k * CH
            col = lax.broadcasted_iota(jnp.int32, (CH, rows), 1)
            SII[pl.ds(k, 1), :] = jnp.sum(jnp.where(row == col, d, 0.0), axis=0, keepdims=True)

    def square_piece(h, k, c):
        for t in (1, 2, 3):
            d = scores(t, h, pl.multiple_of(k * CH, CH), CH, pl.multiple_of(c * CH, CH), CH)
            put(2 * t + h, k, chunk(c), d)

    def take_in(i):
        c_q(i).wait_recv()
        c_3(i).start()
        c_y(i).wait_recv()

        @pl.when(even)
        def _():
            c_5(i).start()

    def arrived(lo, hi):
        loop(lo, hi, lambda i: c_3(i).wait_recv())

        @pl.when(even)
        def _():
            loop(lo, hi, lambda i: c_5(i).wait_recv())

    def phase1(x):
        k, j = x // 8, lax.rem(x, 8)
        i, h, kk = lax.rem(j, 3), j // 3, k - 1
        loop(x * per // 8, (x + 1) * per // 8, take_in)

        @pl.when((k == 0) & (j == 3))
        def _():
            c_1().wait_recv()

        @pl.when((k == 0) & (j < 6))
        def _():
            own_piece(h, i)

        @pl.when((k > 0) & (j == 0))
        def _():
            loop(kk * per, k * per, lambda i: c_l(i).wait_recv())

        @pl.when((k > 0) & (j == 3))
        def _():
            arrived(kk * per, k * per)

        @pl.when((k > 0) & (j < 6) & (i < 2 * kk + 1))
        def _():
            square_piece(h, jnp.minimum(i, kk), jnp.where(i < kk, kk, i - kk))

    loop(0, 8 * nk, phase1)
    def join(*parts):
        top = functools.reduce(jnp.maximum, parts)
        return top + jnp.log(sum(jnp.exp(part - top) for part in parts))

    def of_terms(lo, hi):
        m = functools.reduce(jnp.maximum, [MX[k, lo:hi, :] for k in range(nk)])
        return m + jnp.log(sum(SM[k, lo:hi, :] * jnp.exp(MX[k, lo:hi, :] - m) for k in range(nk)))

    def near():
        return [c_sa(0, dev_d), c_sa(1, dev_q), c_sa(2, dev_qd)]

    def far_own():
        return [c_sp(0, 2, (at(-2), n)), c_sp(1, 3, (at(-2), nc))]

    def far_passed():
        return [
            c_sb(1, 1, (at(3), n)), c_sb(2, 2, (at(3), nc)), c_sb(3, 1, (at(2), n)), c_sb(4, 2, (at(2), nc)),
            c_sb(0, 0, dev_d),
        ]

    def far_got():
        return [c_sp(0, 0, (at(-3), n)), c_sp(1, 1, (at(-3), nc))]

    def each(copies, act):
        for copy in copies:
            act(copy)

    @pl.when(even)
    def _():
        SP[...] = of_terms(0, 2)
        each(far_own(), lambda copy: copy.start())

    edge = (nk - 1) * CH

    def last_queries(t, h, upto):
        d = scores(t, h, 0, upto, edge, CH)
        for k in range(upto // CH):
            put(2 * t + h, k, slice(edge, rows), d[k * CH : (k + 1) * CH])

    def last_labels(t, h, upto):
        put(2 * t + h, nk - 1, slice(0, upto), scores(t, h, edge, CH, 0, upto))

    for t in (1, 2, 3):
        last_queries(t, 0, edge)
    loop((nk - 1) * per, ns, lambda i: c_l(i).wait_recv())
    for i in range(3):
        t = jnp.where(even, 1 + i, 1 + (i + 1) % 3)
        last_labels(t, 0, rows)
        last_labels(t, 1, edge)
        if i == 0:
            arrived((nk - 1) * per, ns)
        last_queries(t, 1, rows)
        if i == 0:

            @pl.when(even)
            def _():
                SB[...] = of_terms(2, 4)
                each(far_passed(), lambda copy: copy.start())

        if i == 1:

            @pl.when(odd)
            def _():
                SP[...] = join(of_terms(4, 6), of_terms(6, 8))
                each(far_got(), lambda copy: copy.start())

    def lg_piece(t0, count, c, more=False):
        def term(i):
            t = t0 + i
            row = lax.broadcasted_iota(jnp.int32, (CH, rows), 0) + c * CH
            col = lax.broadcasted_iota(jnp.int32, (CH, rows), 1) + rows * jnp.minimum(t, 1)
            hit = jnp.where(row == col, 1.0, 0.0)
            w0 = (E[2 * t, chunk(c), :] * AL[c, pl.ds(2 * t, 1), :] - hit).astype(BF16)
            w1 = (E[2 * t + 1, chunk(c), :] * AL[c, pl.ds(2 * t + 1, 1), :]).astype(BF16)
            g = lax.dot_general(w0, B[queries_of(t)], NN, preferred_element_type=F32)
            g = g + lax.dot_general(w1, B[queries_of(t) + 1], NN, preferred_element_type=F32)
            if more:
                GT[...] = GT[...] + g
                return

            @pl.when(i == 0)
            def _():
                GT[...] = g

            @pl.when(i > 0)
            def _():
                GT[...] = GT[...] + g

        loop(0, count, term)

    def qg_piece(t0, count, h, c):
        def term(i):
            t = t0 + i
            ts = 2 * t + h
            row = lax.broadcasted_iota(jnp.int32, (CH, CH), 0)
            col = lax.broadcasted_iota(jnp.int32, (CH, CH), 1) + c * CH + rows * jnp.minimum(ts, 1)
            ws = []
            for k in range(nk):
                x = E[ts, chunk(k), chunk(c)] * AL[k, pl.ds(ts, 1), chunk(c)]
                ws.append((x - jnp.where(row + k * CH == col, 1.0, 0.0)).astype(BF16))
            g = lax.dot_general(
                jnp.concatenate(ws, axis=0), B[labels_of(t)], TN, preferred_element_type=F32
            )

            @pl.when(i == 0)
            def _():
                GT[...] = g

            @pl.when(i > 0)
            def _():
                GT[...] = GT[...] + g

        loop(0, count, term)

    of_term = of_terms(0, 8)
    SA[0:2, :] = jnp.where(odd, join(of_term[0:2], of_term[2:4]), of_term[0:2])
    SA[2:4, :] = join(of_term[4:6], of_term[6:8])
    each(near(), lambda copy: copy.start())

    got = SA[2:4, :]
    own_view = jnp.concatenate([of_term[0:4], got, got], axis=0)
    for k in range(nk):
        AL[k] = jnp.exp(MX[k] - own_view)

    def early(i):
        of_got = i != 1

        @pl.when(of_got | even)
        def _():
            qg_piece(jnp.where(of_got, 2, 1), jnp.where(of_got, 2, 1), 1 - i // 2, 0)

        @pl.when(i == 0)
        def _():
            DS3[:CH, :] = GT[...].astype(BF16)
            c_d3(0).start()

        @pl.when((i == 1) & even)
        def _():
            DS5[:CH, :] = GT[...].astype(BF16)
            c_d5(0).start()

        @pl.when(i == 2)
        def _():
            QG0[:CH, :] = GT[...]

    loop(0, 3, early)

    def swap(x):
        return jnp.concatenate([x[1:2], x[0:1]], axis=0)

    def settle(first, pairs):
        lse = jnp.concatenate(pairs, axis=0)
        last = first + lse.shape[0]
        for k in range(nk):
            AL[k, first:last, :] = jnp.exp(MX[k, first:last, :] - lse)

    def send(copy, c):
        loop(c * per, (c + 1) * per, lambda i: copy(i).start())

    each(near(), lambda copy: copy.wait_recv())
    near0 = [SA[0:2, :], swap(RA[0, 0:2, :]), RA[1, 2:4, :], swap(RA[2, 2:4, :])]
    near1 = [SA[2:4, :], swap(RA[0, 2:4, :]), RA[1, 0:2, :], swap(RA[2, 0:2, :])]

    @pl.when(even)
    def _():
        lse1 = join(*near1)
        settle(4, [lse1, lse1])
        TR[4:6, :] = lse1[:, :CH]

    @pl.when(odd)
    def _():
        lse0 = join(*near0)
        settle(0, [lse0, lse0])
        loss_ref[...] = (lse0[0:1] - sum(SII[k : k + 1, :] for k in range(nk))).reshape(rows)

    lg_piece(2 - par, 1, 0)

    for j in (1, 2):
        c_sb(j, j, dev_d).wait_recv()
    far = [RB[1], swap(RB[2])]

    @pl.when(even)
    def _():
        for j in range(4):
            c_sp(j, j, dev_d).wait_recv()
        c_sb(0, 0, dev_d).wait_recv()
        lse0 = join(*near0, *far)
        lse2 = join(SB[...], swap(RB[0]), RP[0], swap(RP[1]), RP[2], swap(RP[3]))
        settle(0, [lse0, lse2])
        loss_ref[...] = (lse0[0:1] - sum(SII[k : k + 1, :] for k in range(nk))).reshape(rows)
        TR[2:3, :] = jnp.exp(RB[0, 1:2, :CH] - lse2[0:1, :CH])

    @pl.when(odd)
    def _():
        lse1 = join(*near1, *far)
        settle(4, [lse1, lse1])
        TR[4:6, :] = lse1[:, :CH]

    lg_piece(1 + par, 1, 0, more=True)
    LS[:CH, :] = GT[...].astype(BF16)
    send(c_lz, 0)

    TR[0:1, :] = jnp.exp(SA[2:3, :CH] - TR[4:5, :])
    TR[1:2, :] = jnp.exp(RA[0, 3:4, :CH] - TR[4:5, :])
    column = jnp.transpose(TR[...])

    @pl.when(even)
    def _():
        qg_piece(1, 1, 0, 0)
        c_d5(0).wait_recv()
        YS[:CH, :] = (GT[...] + DR4[:CH, :].astype(F32) * column[:, 2:3]).astype(BF16)
        send(c_yr, 0)

    @pl.when(odd)
    def _():
        lg_piece(3, 1, 0)
        YS[:CH, :] = GT[...].astype(BF16)
        send(c_yr, 0)

    c_d3(0).wait_recv()
    QS[:CH, :] = (QG0[:CH, :] * column[:, 0:1] + DR2[:CH, :].astype(F32) * column[:, 1:2]).astype(BF16)
    send(c_qz, 0)

    def phase3(x):
        first = x < 5 * nk
        y = x - 5 * nk
        c = jnp.where(first, x // 5, y // 4)
        v = jnp.where(first, lax.rem(x, 5), 6 + lax.rem(y + 8 * nk, 4))
        later = (c > 0) | (v >= 6)
        lg = ((v == 2) & later) | (v == 7) | ((v == 1) & odd & later) | ((v == 8) & even)
        qg = later & ((v == 0) | (v == 3) | (v == 6) | (v == 9) | (((v == 1) | (v == 4)) & even))

        @pl.when(lg)
        def _():
            t0 = jnp.where(v == 2, 1, jnp.where(v == 7, 0, 3))
            lg_piece(t0, jnp.where(v == 2, 2, 1), c)

        @pl.when(qg)
        def _():
            passed = (v == 1) | (v == 4)
            t0 = jnp.where(passed, 1, jnp.where(v >= 6, 0, 2))
            count = jnp.where(passed, 1, jnp.where(v >= 6, 1 + par, 2))
            qg_piece(t0, count, jnp.where((v == 0) | (v == 1) | (v == 6), 1, 0), c)

        @pl.when((v == 0) & later)
        def _():
            DS3[chunk(c), :] = GT[...].astype(BF16)
            c_d3(c).start()

        @pl.when((v == 1) & even & later)
        def _():
            DS5[chunk(c), :] = GT[...].astype(BF16)
            c_d5(c).start()

        @pl.when((v == 1) & odd & later)
        def _():
            YS[chunk(c), :] = GT[...].astype(BF16)
            send(c_yr, c)

        @pl.when((v == 2) & later)
        def _():
            LS[chunk(c), :] = GT[...].astype(BF16)
            send(c_lz, c)

        @pl.when((v == 3) & later)
        def _():
            c_d3(c).wait_recv()
            QS[chunk(c), :] = (GT[...] + DR2[chunk(c), :].astype(F32)).astype(BF16)
            send(c_qz, c)

        @pl.when((v == 4) & even & later)
        def _():
            c_d5(c).wait_recv()
            YS[chunk(c), :] = (GT[...] + DR4[chunk(c), :].astype(F32)).astype(BF16)
            send(c_yr, c)

        @pl.when(v == 6)
        def _():
            DS1[chunk(c), :] = GT[...].astype(BF16)
            c_d1(c).start()

        @pl.when(v == 7)
        def _():
            ACC[chunk(c), :] = GT[...]

        @pl.when((v == 8) & even)
        def _():
            ACC[chunk(c), :] = ACC[chunk(c), :] + GT[...]

        @pl.when(v == 9)
        def _():
            QG0[chunk(c), :] = GT[...]

    loop(0, 9 * nk, phase3)

    def drain(i):
        for copy in (c_q, c_l, c_y, c_3):
            copy(i).wait_send()

        @pl.when(even)
        def _():
            c_5(i).wait_send()

    loop(0, ns, drain)
    c_1().wait_send()
    each(near(), lambda copy: copy.wait_send())
    pl.when(even)(lambda: each(far_own() + far_passed(), lambda copy: copy.wait_send()))
    pl.when(odd)(lambda: each(far_got(), lambda copy: copy.wait_send()))

    def drain_cores(c):
        c_d1(c).wait_recv()
        c_d3(c).wait_send()
        c_d1(c).wait_send()

        @pl.when(even)
        def _():
            c_d5(c).wait_send()

    loop(0, nk, drain_cores)

    def finish(i):
        for copy in (c_yr, c_qz, c_lz):
            copy(i).wait_send()
        c_yr(i).wait_recv()
        passed = YR[sub(i), :].astype(F32)
        c_qz(i).wait_recv()
        g = QG0[sub(i), :] + DR0[sub(i), :].astype(F32) + jnp.where(even, passed, 0.0)
        qg_ref[sub(i), :] = (g + QR[sub(i), :].astype(F32)).astype(BF16)
        c_lz(i).wait_recv()
        g = ACC[sub(i), :] + jnp.where(odd, passed, 0.0)
        lg_ref[sub(i), :] = (g + LR[sub(i), :].astype(F32)).astype(BF16)

    loop(0, ns, finish)


def hand_over_kernel(*refs):
    ins, outs, sems = refs[:3], refs[3:6], refs[6]
    copies = [pltpu.make_async_copy(ins[0], outs[0], sems.at[0, 0])]
    step = ins[1].shape[0] // PARTS
    for j in (1, 2):
        for i in range(PARTS):
            part = pl.ds(i * step, step)
            copies.append(pltpu.make_async_copy(ins[j].at[part], outs[j].at[part], sems.at[j, i]))
    for copy in copies:
        copy.start()
    for copy in copies:
        copy.wait()


def hand_over(*results):
    return pl.pallas_call(
        hand_over_kernel,
        out_shape=tuple(jax.ShapeDtypeStruct(x.shape, x.dtype) for x in results),
        in_specs=[pl.BlockSpec(memory_space=pltpu.VMEM)] * 3,
        out_specs=(pl.BlockSpec(memory_space=pltpu.HBM),) * 3,
        scratch_shapes=[pltpu.SemaphoreType.DMA((3, PARTS))],
        compiler_params=pltpu.CompilerParams(vmem_limit_bytes=4 * 2**20),
    )(*results)


def local(queries, labels, logit_scale):
    rows, width = queries.shape
    nk, ns = rows // CH, rows // SUB
    block = (rows, width)
    dma = pltpu.SemaphoreType.DMA
    counts = [ns, ns, ns, 1, ns, ns, 3, 5, 4, ns, ns, ns, nk, nk, nk]
    loss, query_grad, label_grad = pl.pallas_call(
        kernel,
        out_shape=(
            jax.ShapeDtypeStruct((rows,), F32),
            jax.ShapeDtypeStruct(block, BF16),
            jax.ShapeDtypeStruct(block, BF16),
        ),
        in_specs=[
            pl.BlockSpec(memory_space=pltpu.SMEM),
            pl.BlockSpec(memory_space=pltpu.HBM),
            pl.BlockSpec(memory_space=pltpu.HBM),
        ],
        out_specs=(pl.BlockSpec(memory_space=pltpu.VMEM),) * 3,
        scratch_shapes=[
            pltpu.VMEM((8, *block), BF16),
            pltpu.VMEM((8, rows, rows), F32),
            pltpu.VMEM((nk, 8, rows), F32),
            pltpu.VMEM((nk, 8, rows), F32),
            pltpu.VMEM((nk, 8, rows), F32),
            pltpu.VMEM((4, rows), F32),
            pltpu.VMEM((2, rows), F32),
            pltpu.VMEM((2, rows), F32),
            pltpu.VMEM((3, 4, rows), F32),
            pltpu.VMEM((3, 2, rows), F32),
            pltpu.VMEM((4, 2, rows), F32),
            pltpu.VMEM((8, rows), F32),
            pltpu.VMEM((8, CH), F32),
            pltpu.VMEM(block, F32),
            pltpu.VMEM(block, F32),
            pltpu.VMEM((CH, width), F32),
            *[pltpu.VMEM(block, BF16)] * 12,
            dma((2,)),
            *[dma((count,)) for count in counts for _ in range(2)],
        ],
        compiler_params=pltpu.CompilerParams(
            collective_id=0, has_side_effects=True, vmem_limit_bytes=51 * 2**20
        ),
        cost_estimate=pl.CostEstimate(
            flops=6 * rows * 8 * rows * width, bytes_accessed=8 * rows * width, transcendentals=8 * rows * rows
        ),
    )(logit_scale, queries, labels)
    return hand_over(loss, query_grad, label_grad)


def solution(mesh):
    in_specs = (P(("wide", "narrow"), None), P(("wide", "narrow"), None), P())
    out_specs = (P(("wide", "narrow")), P(("wide", "narrow"), None), P(("wide", "narrow"), None))
    return jax.shard_map(local, mesh=mesh, in_specs=in_specs, out_specs=out_specs, check_vma=False)
```

```python
import functools
import math

import jax
import jax.numpy as jnp
from jax import lax
from jax.experimental import pallas as pl
from jax.experimental.pallas import tpu as pltpu
from jax.sharding import PartitionSpec as P

MESH = pl.DeviceIdType.MESH
F32, BF16 = jnp.float32, jnp.bfloat16
CH = 256
SUB = 128
PARTS = 4
NT = (((1,), (1,)), ((), ()))
NN = (((1,), (0,)), ((), ()))
TN = (((0,), (0,)), ((), ()))
OWN_Q, GOT_Q, PASSED, OWN_L, GOT_L = 0, 2, 4, 6, 7


def kernel(
    scale_ref, q_ref, l_ref, loss_ref, qg_ref, lg_ref,
    B, E, MX, SM, AL, SA, SB, SP, RA, RB, RP, SII, TR, ACC, QG0, GT,
    YS, LS, QS, DS3, DS5, DS1, YR, LR, QR, DR2, DR4, DR0,
    s_in, s_q, r_q, s_l, r_l, s_y, r_y, s_1, r_1, s_3, r_3, s_5, r_5, s_sa, r_sa, s_sb, r_sb, s_sp, r_sp,
    s_yr, r_yr, s_qz, r_qz, s_lz, r_lz, s_d3, r_d3, s_d5, r_d5, s_d1, r_d1,
):
    rows = q_ref.shape[0]
    nk, ns = rows // CH, rows // SUB
    per = CH // SUB
    w, n = lax.axis_index("wide"), lax.axis_index("narrow")
    nw = lax.axis_size("wide")
    par = lax.rem(w, 2)
    even, odd = par == 0, par == 1
    wx = w + 1 - 2 * par
    nc = n + 1 - 2 * lax.rem(n, 2)

    def at(step):
        return lax.rem(w + nw + step, nw)

    dev_q, dev_l = (wx, n), (wx, lax.rem(n + 2, 4))
    dev_d, dev_qd = (w, nc), (wx, nc)
    out_y = (at(4 * par - 2), n)
    back_y = (at(2 - 4 * par), n)
    factor = scale_ref[0] * (1.0 / math.sqrt(q_ref.shape[1]))

    def sub(i):
        return pl.ds(pl.multiple_of(i * SUB, SUB), SUB)

    def chunk(c):
        return pl.ds(pl.multiple_of(c * CH, CH), CH)

    def rc(src, dst, ssem, rsem, dev):
        return pltpu.make_async_remote_copy(
            src_ref=src, dst_ref=dst, send_sem=ssem, recv_sem=rsem, device_id=dev, device_id_type=MESH
        )

    def c_q(i):
        return rc(q_ref.at[sub(i)], B.at[GOT_Q, sub(i)], s_q.at[i], r_q.at[i], dev_q)

    def c_l(i):
        return rc(l_ref.at[sub(i)], B.at[GOT_L, sub(i)], s_l.at[i], r_l.at[i], dev_l)

    def c_y(i):
        return rc(B.at[OWN_L * par, sub(i)], B.at[PASSED, sub(i)], s_y.at[i], r_y.at[i], out_y)

    def c_1():
        return rc(q_ref, B.at[OWN_Q + 1], s_1.at[0], r_1.at[0], dev_d)

    def c_3(i):
        return rc(B.at[GOT_Q, sub(i)], B.at[GOT_Q + 1, sub(i)], s_3.at[i], r_3.at[i], dev_d)

    def c_5(i):
        return rc(B.at[PASSED, sub(i)], B.at[PASSED + 1, sub(i)], s_5.at[i], r_5.at[i], dev_d)

    def c_sa(j, dev):
        return rc(SA, RA.at[j], s_sa.at[j], r_sa.at[j], dev)

    def c_sp(i, j, dev):
        return rc(SP, RP.at[j], s_sp.at[i], r_sp.at[j], dev)

    def c_sb(i, j, dev):
        return rc(SB, RB.at[j], s_sb.at[i], r_sb.at[j], dev)

    def c_yr(i):
        return rc(YS.at[sub(i)], YR.at[sub(i)], s_yr.at[i], r_yr.at[i], back_y)

    def c_qz(i):
        return rc(QS.at[sub(i)], QR.at[sub(i)], s_qz.at[i], r_qz.at[i], dev_q)

    def c_lz(i):
        return rc(LS.at[sub(i)], LR.at[sub(i)], s_lz.at[i], r_lz.at[i], dev_l)

    def c_d3(c):
        return rc(DS3.at[chunk(c)], DR2.at[chunk(c)], s_d3.at[c], r_d3.at[c], dev_d)

    def c_d5(c):
        return rc(DS5.at[chunk(c)], DR4.at[chunk(c)], s_d5.at[c], r_d5.at[c], dev_d)

    def c_d1(c):
        return rc(DS1.at[chunk(c)], DR0.at[chunk(c)], s_d1.at[c], r_d1.at[c], dev_d)

    def loop(lo, hi, body):
        def step(i, carry):
            body(i)
            return carry

        lax.fori_loop(lo, hi, step, 0)

    in_q = pltpu.make_async_copy(q_ref, B.at[OWN_Q], s_in.at[0])
    in_l = pltpu.make_async_copy(l_ref, B.at[OWN_L], s_in.at[1])
    in_q.start()
    in_l.start()
    barrier = pltpu.get_barrier_semaphore()
    for dev in (back_y, dev_l, dev_q, dev_qd, dev_d):
        pl.semaphore_signal(barrier, inc=1, device_id=dev, device_id_type=MESH)
    in_q.wait()
    in_l.wait()
    pl.semaphore_wait(barrier, 5)

    def send_first(i):
        c_y(i).start()
        c_l(i).start()
        c_q(i).start()

    loop(0, ns, send_first)
    c_1().start()

    def labels_of(t):
        return jnp.where(t == 0, OWN_L, jnp.where(t == 3, OWN_L - 2 * par, GOT_L))

    def queries_of(t):
        return jnp.where(t == 0, OWN_Q, jnp.where(t == 1, PASSED - PASSED * par, GOT_Q))

    def scores(t, h, row0, height, col0, width):
        lab = B[labels_of(t), pl.ds(row0, height), :]
        qry = B[queries_of(t) + h, pl.ds(col0, width), :]
        return lax.dot_general(lab, qry, NT, preferred_element_type=F32) * factor

    def put(ts, k, cols, d):
        m = jnp.max(d, axis=0, keepdims=True)
        e = jnp.exp(d - m)
        E[ts, chunk(k), cols] = e
        MX[k, pl.ds(ts, 1), cols] = m
        SM[k, pl.ds(ts, 1), cols] = jnp.sum(e, axis=0, keepdims=True)

    def own_piece(h, k):
        d = scores(0, h, pl.multiple_of(k * CH, CH), CH, 0, rows)
        put(h, k, slice(None), d)

        @pl.when(h == 0)
        def _():
            row = lax.broadcasted_iota(jnp.int32, (CH, rows), 0) + k * CH
            col = lax.broadcasted_iota(jnp.int32, (CH, rows), 1)
            SII[pl.ds(k, 1), :] = jnp.sum(jnp.where(row == col, d, 0.0), axis=0, keepdims=True)

    def square_piece(h, k, c):
        for t in (1, 2, 3):
            d = scores(t, h, pl.multiple_of(k * CH, CH), CH, pl.multiple_of(c * CH, CH), CH)
            put(2 * t + h, k, chunk(c), d)

    def take_in(i):
        c_q(i).wait_recv()
        c_3(i).start()
        c_y(i).wait_recv()

        @pl.when(even)
        def _():
            c_5(i).start()

    def arrived(lo, hi):
        loop(lo, hi, lambda i: c_3(i).wait_recv())

        @pl.when(even)
        def _():
            loop(lo, hi, lambda i: c_5(i).wait_recv())

    def phase1(x):
        k, j = x // 8, lax.rem(x, 8)
        i, h, kk = lax.rem(j, 3), j // 3, k - 1
        loop(x * per // 8, (x + 1) * per // 8, take_in)

        @pl.when((k == 0) & (j == 3))
        def _():
            c_1().wait_recv()

        @pl.when((k == 0) & (j < 6))
        def _():
            own_piece(h, i)

        @pl.when((k > 0) & (j == 0))
        def _():
            loop(kk * per, k * per, lambda i: c_l(i).wait_recv())

        @pl.when((k > 0) & (j == 3))
        def _():
            arrived(kk * per, k * per)

        @pl.when((k > 0) & (j < 6) & (i < 2 * kk + 1))
        def _():
            square_piece(h, jnp.minimum(i, kk), jnp.where(i < kk, kk, i - kk))

    loop(0, 8 * nk, phase1)
    def join(*parts):
        top = functools.reduce(jnp.maximum, parts)
        return top + jnp.log(sum(jnp.exp(part - top) for part in parts))

    def of_terms(lo, hi):
        m = functools.reduce(jnp.maximum, [MX[k, lo:hi, :] for k in range(nk)])
        return m + jnp.log(sum(SM[k, lo:hi, :] * jnp.exp(MX[k, lo:hi, :] - m) for k in range(nk)))

    def near():
        return [c_sa(0, dev_d), c_sa(1, dev_q), c_sa(2, dev_qd)]

    def far_own():
        return [c_sp(0, 2, (at(-2), n)), c_sp(1, 3, (at(-2), nc))]

    def far_passed():
        return [
            c_sb(1, 1, (at(3), n)), c_sb(2, 2, (at(3), nc)), c_sb(3, 1, (at(2), n)), c_sb(4, 2, (at(2), nc)),
            c_sb(0, 0, dev_d),
        ]

    def far_got():
        return [c_sp(0, 0, (at(-3), n)), c_sp(1, 1, (at(-3), nc))]

    def each(copies, act):
        for copy in copies:
            act(copy)

    @pl.when(even)
    def _():
        SP[...] = of_terms(0, 2)
        each(far_own(), lambda copy: copy.start())

    edge = (nk - 1) * CH

    def last_queries(t, h, upto):
        d = scores(t, h, 0, upto, edge, CH)
        for k in range(upto // CH):
            put(2 * t + h, k, slice(edge, rows), d[k * CH : (k + 1) * CH])

    def last_labels(t, h, upto):
        put(2 * t + h, nk - 1, slice(0, upto), scores(t, h, edge, CH, 0, upto))

    for t in (1, 2, 3):
        last_queries(t, 0, edge)
    loop((nk - 1) * per, ns, lambda i: c_l(i).wait_recv())
    for i in range(3):
        t = jnp.where(even, 1 + i, 1 + (i + 1) % 3)
        last_labels(t, 0, rows)
        last_labels(t, 1, edge)
        if i == 0:
            arrived((nk - 1) * per, ns)
        last_queries(t, 1, rows)
        if i == 0:

            @pl.when(even)
            def _():
                SB[...] = of_terms(2, 4)
                each(far_passed(), lambda copy: copy.start())

        if i == 1:

            @pl.when(odd)
            def _():
                SP[...] = join(of_terms(4, 6), of_terms(6, 8))
                each(far_got(), lambda copy: copy.start())

    def lg_piece(t0, count, c, more=False):
        def term(i):
            t = t0 + i
            row = lax.broadcasted_iota(jnp.int32, (CH, rows), 0) + c * CH
            col = lax.broadcasted_iota(jnp.int32, (CH, rows), 1) + rows * jnp.minimum(t, 1)
            hit = jnp.where(row == col, 1.0, 0.0)
            w0 = (E[2 * t, chunk(c), :] * AL[c, pl.ds(2 * t, 1), :] - hit).astype(BF16)
            w1 = (E[2 * t + 1, chunk(c), :] * AL[c, pl.ds(2 * t + 1, 1), :]).astype(BF16)
            g = lax.dot_general(w0, B[queries_of(t)], NN, preferred_element_type=F32)
            g = g + lax.dot_general(w1, B[queries_of(t) + 1], NN, preferred_element_type=F32)
            if more:
                GT[...] = GT[...] + g
                return

            @pl.when(i == 0)
            def _():
                GT[...] = g

            @pl.when(i > 0)
            def _():
                GT[...] = GT[...] + g

        loop(0, count, term)

    def qg_piece(t0, count, h, c):
        def term(i):
            t = t0 + i
            ts = 2 * t + h
            row = lax.broadcasted_iota(jnp.int32, (CH, CH), 0)
            col = lax.broadcasted_iota(jnp.int32, (CH, CH), 1) + c * CH + rows * jnp.minimum(ts, 1)
            ws = []
            for k in range(nk):
                x = E[ts, chunk(k), chunk(c)] * AL[k, pl.ds(ts, 1), chunk(c)]
                ws.append((x - jnp.where(row + k * CH == col, 1.0, 0.0)).astype(BF16))
            g = lax.dot_general(
                jnp.concatenate(ws, axis=0), B[labels_of(t)], TN, preferred_element_type=F32
            )

            @pl.when(i == 0)
            def _():
                GT[...] = g

            @pl.when(i > 0)
            def _():
                GT[...] = GT[...] + g

        loop(0, count, term)

    of_term = of_terms(0, 8)
    SA[0:2, :] = jnp.where(odd, join(of_term[0:2], of_term[2:4]), of_term[0:2])
    SA[2:4, :] = join(of_term[4:6], of_term[6:8])
    each(near(), lambda copy: copy.start())

    got = SA[2:4, :]
    own_view = jnp.concatenate([of_term[0:4], got, got], axis=0)
    for k in range(nk):
        AL[k] = jnp.exp(MX[k] - own_view)

    def early(i):
        of_got = i != 1

        @pl.when(of_got | even)
        def _():
            qg_piece(jnp.where(of_got, 2, 1), jnp.where(of_got, 2, 1), 1 - i // 2, 0)

        @pl.when(i == 0)
        def _():
            DS3[:CH, :] = GT[...].astype(BF16)
            c_d3(0).start()

        @pl.when((i == 1) & even)
        def _():
            DS5[:CH, :] = GT[...].astype(BF16)
            c_d5(0).start()

        @pl.when(i == 2)
        def _():
            QG0[:CH, :] = GT[...]

    loop(0, 3, early)

    def swap(x):
        return jnp.concatenate([x[1:2], x[0:1]], axis=0)

    def settle(first, pairs):
        lse = jnp.concatenate(pairs, axis=0)
        last = first + lse.shape[0]
        for k in range(nk):
            AL[k, first:last, :] = jnp.exp(MX[k, first:last, :] - lse)

    def send(copy, c):
        loop(c * per, (c + 1) * per, lambda i: copy(i).start())

    each(near(), lambda copy: copy.wait_recv())
    near0 = [SA[0:2, :], swap(RA[0, 0:2, :]), RA[1, 2:4, :], swap(RA[2, 2:4, :])]
    near1 = [SA[2:4, :], swap(RA[0, 2:4, :]), RA[1, 0:2, :], swap(RA[2, 0:2, :])]

    @pl.when(even)
    def _():
        lse1 = join(*near1)
        settle(4, [lse1, lse1])
        TR[4:6, :] = lse1[:, :CH]

    @pl.when(odd)
    def _():
        lse0 = join(*near0)
        settle(0, [lse0, lse0])
        loss_ref[...] = (lse0[0:1] - sum(SII[k : k + 1, :] for k in range(nk))).reshape(rows)

    lg_piece(2 - par, 1, 0)

    for j in (1, 2):
        c_sb(j, j, dev_d).wait_recv()
    far = [RB[1], swap(RB[2])]

    @pl.when(even)
    def _():
        for j in range(4):
            c_sp(j, j, dev_d).wait_recv()
        c_sb(0, 0, dev_d).wait_recv()
        lse0 = join(*near0, *far)
        lse2 = join(SB[...], swap(RB[0]), RP[0], swap(RP[1]), RP[2], swap(RP[3]))
        settle(0, [lse0, lse2])
        loss_ref[...] = (lse0[0:1] - sum(SII[k : k + 1, :] for k in range(nk))).reshape(rows)
        TR[2:3, :] = jnp.exp(RB[0, 1:2, :CH] - lse2[0:1, :CH])

    @pl.when(odd)
    def _():
        lse1 = join(*near1, *far)
        settle(4, [lse1, lse1])
        TR[4:6, :] = lse1[:, :CH]

    lg_piece(1 + par, 1, 0, more=True)
    LS[:CH, :] = GT[...].astype(BF16)
    send(c_lz, 0)

    TR[0:1, :] = jnp.exp(SA[2:3, :CH] - TR[4:5, :])
    TR[1:2, :] = jnp.exp(RA[0, 3:4, :CH] - TR[4:5, :])
    column = jnp.transpose(TR[...])

    @pl.when(even)
    def _():
        qg_piece(1, 1, 0, 0)
        c_d5(0).wait_recv()
        YS[:CH, :] = (GT[...] + DR4[:CH, :].astype(F32) * column[:, 2:3]).astype(BF16)
        send(c_yr, 0)

    @pl.when(odd)
    def _():
        lg_piece(3, 1, 0)
        YS[:CH, :] = GT[...].astype(BF16)
        send(c_yr, 0)

    c_d3(0).wait_recv()
    QS[:CH, :] = (QG0[:CH, :] * column[:, 0:1] + DR2[:CH, :].astype(F32) * column[:, 1:2]).astype(BF16)
    send(c_qz, 0)

    def phase3(x):
        first = x < 5 * nk
        y = x - 5 * nk
        c = jnp.where(first, x // 5, y // 4)
        v = jnp.where(first, lax.rem(x, 5), 6 + lax.rem(y + 8 * nk, 4))
        later = (c > 0) | (v >= 6)
        lg = ((v == 2) & later) | (v == 7) | ((v == 1) & odd & later) | ((v == 8) & even)
        qg = later & ((v == 0) | (v == 3) | (v == 6) | (v == 9) | (((v == 1) | (v == 4)) & even))

        @pl.when(lg)
        def _():
            t0 = jnp.where(v == 2, 1, jnp.where(v == 7, 0, 3))
            lg_piece(t0, jnp.where(v == 2, 2, 1), c)

        @pl.when(qg)
        def _():
            passed = (v == 1) | (v == 4)
            t0 = jnp.where(passed, 1, jnp.where(v >= 6, 0, 2))
            count = jnp.where(passed, 1, jnp.where(v >= 6, 1 + par, 2))
            qg_piece(t0, count, jnp.where((v == 0) | (v == 1) | (v == 6), 1, 0), c)

        @pl.when((v == 0) & later)
        def _():
            DS3[chunk(c), :] = GT[...].astype(BF16)
            c_d3(c).start()

        @pl.when((v == 1) & even & later)
        def _():
            DS5[chunk(c), :] = GT[...].astype(BF16)
            c_d5(c).start()

        @pl.when((v == 1) & odd & later)
        def _():
            YS[chunk(c), :] = GT[...].astype(BF16)
            send(c_yr, c)

        @pl.when((v == 2) & later)
        def _():
            LS[chunk(c), :] = GT[...].astype(BF16)
            send(c_lz, c)

        @pl.when((v == 3) & later)
        def _():
            c_d3(c).wait_recv()
            QS[chunk(c), :] = (GT[...] + DR2[chunk(c), :].astype(F32)).astype(BF16)
            send(c_qz, c)

        @pl.when((v == 4) & even & later)
        def _():
            c_d5(c).wait_recv()
            YS[chunk(c), :] = (GT[...] + DR4[chunk(c), :].astype(F32)).astype(BF16)
            send(c_yr, c)

        @pl.when(v == 6)
        def _():
            DS1[chunk(c), :] = GT[...].astype(BF16)
            c_d1(c).start()

        @pl.when(v == 7)
        def _():
            ACC[chunk(c), :] = GT[...]

        @pl.when((v == 8) & even)
        def _():
            ACC[chunk(c), :] = ACC[chunk(c), :] + GT[...]

        @pl.when(v == 9)
        def _():
            QG0[chunk(c), :] = GT[...]

    loop(0, 9 * nk, phase3)

    def drain(i):
        for copy in (c_q, c_l, c_y, c_3):
            copy(i).wait_send()

        @pl.when(even)
        def _():
            c_5(i).wait_send()

    loop(0, ns, drain)
    c_1().wait_send()
    each(near(), lambda copy: copy.wait_send())
    pl.when(even)(lambda: each(far_own() + far_passed(), lambda copy: copy.wait_send()))
    pl.when(odd)(lambda: each(far_got(), lambda copy: copy.wait_send()))

    def drain_cores(c):
        c_d1(c).wait_recv()
        c_d3(c).wait_send()
        c_d1(c).wait_send()

        @pl.when(even)
        def _():
            c_d5(c).wait_send()

    loop(0, nk, drain_cores)

    def finish(i):
        for copy in (c_yr, c_qz, c_lz):
            copy(i).wait_send()
        c_yr(i).wait_recv()
        passed = YR[sub(i), :].astype(F32)
        c_qz(i).wait_recv()
        g = QG0[sub(i), :] + DR0[sub(i), :].astype(F32) + jnp.where(even, passed, 0.0)
        qg_ref[sub(i), :] = (g + QR[sub(i), :].astype(F32)).astype(BF16)
        c_lz(i).wait_recv()
        g = ACC[sub(i), :] + jnp.where(odd, passed, 0.0)
        lg_ref[sub(i), :] = (g + LR[sub(i), :].astype(F32)).astype(BF16)

    loop(0, ns, finish)


def hand_over_kernel(*refs):
    ins, outs, sems = refs[:3], refs[3:6], refs[6]
    copies = [pltpu.make_async_copy(ins[0], outs[0], sems.at[0, 0])]
    step = ins[1].shape[0] // PARTS
    for j in (1, 2):
        for i in range(PARTS):
            part = pl.ds(i * step, step)
            copies.append(pltpu.make_async_copy(ins[j].at[part], outs[j].at[part], sems.at[j, i]))
    for copy in copies:
        copy.start()
    for copy in copies:
        copy.wait()


def hand_over(*results):
    return pl.pallas_call(
        hand_over_kernel,
        out_shape=tuple(jax.ShapeDtypeStruct(x.shape, x.dtype) for x in results),
        in_specs=[pl.BlockSpec(memory_space=pltpu.VMEM)] * 3,
        out_specs=(pl.BlockSpec(memory_space=pltpu.HBM),) * 3,
        scratch_shapes=[pltpu.SemaphoreType.DMA((3, PARTS))],
        compiler_params=pltpu.CompilerParams(vmem_limit_bytes=4 * 2**20),
    )(*results)


def local(queries, labels, logit_scale):
    rows, width = queries.shape
    nk, ns = rows // CH, rows // SUB
    block = (rows, width)
    dma = pltpu.SemaphoreType.DMA
    counts = [ns, ns, ns, 1, ns, ns, 3, 5, 4, ns, ns, ns, nk, nk, nk]
    loss, query_grad, label_grad = pl.pallas_call(
        kernel,
        out_shape=(
            jax.ShapeDtypeStruct((rows,), F32),
            jax.ShapeDtypeStruct(block, BF16),
            jax.ShapeDtypeStruct(block, BF16),
        ),
        in_specs=[
            pl.BlockSpec(memory_space=pltpu.SMEM),
            pl.BlockSpec(memory_space=pltpu.HBM),
            pl.BlockSpec(memory_space=pltpu.HBM),
        ],
        out_specs=(pl.BlockSpec(memory_space=pltpu.VMEM),) * 3,
        scratch_shapes=[
            pltpu.VMEM((8, *block), BF16),
            pltpu.VMEM((8, rows, rows), F32),
            pltpu.VMEM((nk, 8, rows), F32),
            pltpu.VMEM((nk, 8, rows), F32),
            pltpu.VMEM((nk, 8, rows), F32),
            pltpu.VMEM((4, rows), F32),
            pltpu.VMEM((2, rows), F32),
            pltpu.VMEM((2, rows), F32),
            pltpu.VMEM((3, 4, rows), F32),
            pltpu.VMEM((3, 2, rows), F32),
            pltpu.VMEM((4, 2, rows), F32),
            pltpu.VMEM((8, rows), F32),
            pltpu.VMEM((8, CH), F32),
            pltpu.VMEM(block, F32),
            pltpu.VMEM(block, F32),
            pltpu.VMEM((CH, width), F32),
            *[pltpu.VMEM(block, BF16)] * 12,
            dma((2,)),
            *[dma((count,)) for count in counts for _ in range(2)],
        ],
        compiler_params=pltpu.CompilerParams(
            collective_id=0, has_side_effects=True, vmem_limit_bytes=51 * 2**20
        ),
        cost_estimate=pl.CostEstimate(
            flops=6 * rows * 8 * rows * width, bytes_accessed=8 * rows * width, transcendentals=8 * rows * rows
        ),
    )(logit_scale, queries, labels)
    return hand_over(loss, query_grad, label_grad)


def solution(mesh):
    in_specs = (P(("wide", "narrow"), None), P(("wide", "narrow"), None), P())
    out_specs = (P(("wide", "narrow")), P(("wide", "narrow"), None), P(("wide", "narrow"), None))
    return jax.shard_map(local, mesh=mesh, in_specs=in_specs, out_specs=out_specs, check_vma=False)
```
